256 devices in a mesh: ctx: 64 (over z, y, x_hi), tp: 4 (over x_lo, core).
Axes of the slice: x: 4 (x_hi: 2, x_lo: 2; x = x_hi * 2 + x_lo), y: 4, z: 8, core: 2. Of those that a mesh axis runs over, the one named last changes fastest.
Arguments:
- inputs: bfloat16 [8192, 4096], P('ctx', 'tp'), may hold values from -6 to 6
- out_grad: bfloat16 [8192, 4096], P('ctx', 'tp'), may hold values from -6 to 6
- w_query: bfloat16 [4096, 2048], P(None, 'tp'), may hold values from -0.09375 to 0.09375
- key_weight: bfloat16 [4096, 512], P(None, 'tp'), may hold values from -0.09375 to 0.09375
- value_weight: bfloat16 [4096, 512], P(None, 'tp'), may hold values from -0.09375 to 0.09375
- w_output: bfloat16 [2048, 4096], P('tp'), may hold values from -0.09375 to 0.09375
- times: int32 [8192], replicated, may hold values from 0 to 8191, as said below
Outputs:
- input_grad: bfloat16 [8192, 4096], P('ctx', 'tp')
- gradient_keys: bfloat16 [8192, 512], P('ctx', 'tp')
- gradient_values: bfloat16 [8192, 512], P('ctx', 'tp')
The draws below stay inside these ranges and needn't reach their ends.
Inputs may be any that keep to these rules, and one draw needn't show every extreme that they name: Each event's time is its position in the sequence or one less (the first and last events have exactly their positions), so times are nondecreasing and rise by at most 2 from one event to the next; equal times see each other.
All inputs are finite; a program needn't handle non-finite values.
Results may differ from the reference program's by a relative error of at most 0.02.
Values may be sent and summed in bfloat16 or wider, within the bound.
No kernel may reach another device: no remote copies, remote signals or barrier semaphores. Data moves between devices by JAX's collectives and lax.ppermute only.
A program may use at most 128 MiB of HBM per device.

```python
import jax
import jax.numpy as jnp
from jax import lax

MODEL_WIDTH = 4096
HEAD_SIZE = 128
QUERY_HEADS = 16
KEY_VALUE_HEADS = 4
EVENT_TOKENS = 8192


def draw_inputs(key, part):
    key = jax.random.fold_in(key, 11)
    base_key = jax.random.fold_in(key, 0)
    return jnp.clip(jax.random.normal(base_key, (EVENT_TOKENS, MODEL_WIDTH), jnp.float32), -6.0, 6.0).astype(jnp.bfloat16)


def draw_times(key, part):
    key = jax.random.fold_in(key, 23)
    lagged = jax.random.randint(key, (EVENT_TOKENS,), 0, 2, dtype=jnp.int32)
    positions = jnp.arange(EVENT_TOKENS, dtype=jnp.int32)
    lagged = jnp.where((positions == 0) | (positions == EVENT_TOKENS - 1), 0, lagged)
    return (positions - lagged).astype(jnp.int32)


def level_of(rng, extent, pieces, low, high):
    gain, own = 1.0, jax.random.fold_in(rng, 6)
    for position, shards_of in pieces:
        heights = jnp.exp(jax.random.uniform(jax.random.fold_in(own, position), (shards_of,), jnp.float32, low / len(pieces), high / len(pieces)))
        gain = gain * jnp.repeat(heights, extent[position] // shards_of).reshape([-1 if axis == position else 1 for axis in range(len(extent))])
    return gain


def scatter_about(own_key, dims, spread, bound, cuts=(), kind=jnp.bfloat16):
    gain = level_of(own_key, dims, cuts, -0.22, 0.18) if cuts else 1.0
    array = jax.random.normal(own_key, dims, jnp.float32) * spread * gain
    return jnp.minimum(jnp.maximum(array, -bound), bound).astype(kind)


def setup_inputs(seed: int = 0) -> dict:
    seeds = jax.random.split(jax.random.key(seed), 8)
    inputs = draw_inputs(jax.random.fold_in(seeds[7], 71), 0)
    out_grad = scatter_about(seeds[1], (EVENT_TOKENS, MODEL_WIDTH), 1.0, 6.0, ((0, 64), (1, 4)))
    w_query = scatter_about(seeds[2], (MODEL_WIDTH, QUERY_HEADS * HEAD_SIZE), MODEL_WIDTH ** -0.5, 0.09375, ((1, 4),))
    key_weight = scatter_about(seeds[3], (MODEL_WIDTH, KEY_VALUE_HEADS * HEAD_SIZE), MODEL_WIDTH ** -0.5, 0.09375, ((1, 4),))
    value_weight = scatter_about(seeds[4], (MODEL_WIDTH, KEY_VALUE_HEADS * HEAD_SIZE), MODEL_WIDTH ** -0.5, 0.09375, ((1, 4),))
    w_output = scatter_about(seeds[5], (QUERY_HEADS * HEAD_SIZE, MODEL_WIDTH), MODEL_WIDTH ** -0.5, 0.09375, ((0, 4),))
    times = draw_times(jax.random.fold_in(seeds[7], 71), 0)
    return dict(inputs=inputs, out_grad=out_grad, w_query=w_query, key_weight=key_weight, value_weight=value_weight, w_output=w_output, times=times)


def contract_last(left, right):
    return lax.dot_general(left, right, (((1,), (1,)), ((), ())), preferred_element_type=jnp.float32)


def contract_first(left, right):
    return lax.dot_general(left, right, (((0,), (0,)), ((), ())), preferred_element_type=jnp.float32)


def reference(inputs, out_grad, w_query, key_weight, value_weight, w_output, times):
    factor = HEAD_SIZE ** -0.5
    query = jnp.dot(inputs, w_query, preferred_element_type=jnp.float32).astype(jnp.bfloat16)
    key_all = jnp.dot(inputs, key_weight, preferred_element_type=jnp.float32).astype(jnp.bfloat16)
    value_all = jnp.dot(inputs, value_weight, preferred_element_type=jnp.float32).astype(jnp.bfloat16)
    attn_grad = contract_last(out_grad, w_output).astype(jnp.bfloat16)
    visible = times[None, :] <= times[:, None]
    heads_per_group = QUERY_HEADS // KEY_VALUE_HEADS

    def single_group(group_index):
        key_head = lax.dynamic_slice_in_dim(key_all, group_index * HEAD_SIZE, HEAD_SIZE, 1)
        value_head = lax.dynamic_slice_in_dim(value_all, group_index * HEAD_SIZE, HEAD_SIZE, 1)
        key_sum = jnp.zeros((EVENT_TOKENS, HEAD_SIZE), jnp.float32)
        value_sum = jnp.zeros((EVENT_TOKENS, HEAD_SIZE), jnp.float32)
        query_parts = []
        for member in range(heads_per_group):
            head_start = (group_index * heads_per_group + member) * HEAD_SIZE
            query_head = lax.dynamic_slice_in_dim(query, head_start, HEAD_SIZE, 1)
            grad_head = lax.dynamic_slice_in_dim(attn_grad, head_start, HEAD_SIZE, 1)
            scores = contract_last(query_head, key_head) * factor
            scores = jnp.where(visible, scores, -jnp.inf)
            row_top = jnp.max(scores, axis=1, keepdims=True)
            lse = row_top + jnp.log(jnp.sum(jnp.exp(scores - row_top), axis=1, keepdims=True))
            prob = jnp.exp(scores - lse)
            prob_low = prob.astype(jnp.bfloat16)
            attn_out = jnp.dot(prob_low, value_head, preferred_element_type=jnp.float32).astype(jnp.bfloat16)
            delta = jnp.sum(grad_head.astype(jnp.float32) * attn_out.astype(jnp.float32), axis=1, keepdims=True)
            prob_grad = contract_last(grad_head, value_head)
            score_grad = (prob * (prob_grad - delta)).astype(jnp.bfloat16)
            query_parts.append(jnp.dot(score_grad, key_head, preferred_element_type=jnp.float32) * factor)
            key_sum = key_sum + contract_first(score_grad, query_head)
            value_sum = value_sum + contract_first(prob_low, grad_head)
        gradient_queries = jnp.concatenate(query_parts, axis=1).astype(jnp.bfloat16)
        return gradient_queries, (key_sum * factor).astype(jnp.bfloat16), value_sum.astype(jnp.bfloat16)

    gradient_queries, gradient_keys, gradient_values = lax.map(single_group, jnp.arange(KEY_VALUE_HEADS, dtype=jnp.int32))
    gradient_queries = jnp.transpose(gradient_queries, (1, 0, 2)).reshape(EVENT_TOKENS, QUERY_HEADS * HEAD_SIZE)
    gradient_keys = jnp.transpose(gradient_keys, (1, 0, 2)).reshape(EVENT_TOKENS, KEY_VALUE_HEADS * HEAD_SIZE)
    gradient_values = jnp.transpose(gradient_values, (1, 0, 2)).reshape(EVENT_TOKENS, KEY_VALUE_HEADS * HEAD_SIZE)
    total = contract_last(gradient_queries, w_query) + contract_last(gradient_keys, key_weight) + contract_last(gradient_values, value_weight)
    return total.astype(jnp.bfloat16), gradient_keys, gradient_values
```

```python
import functools

import jax
import jax.numpy as jnp
from jax import lax
from jax.experimental import pallas as pl
from jax.experimental.pallas import tpu as pltpu
from jax.sharding import Mesh
from jax.sharding import PartitionSpec as P

HEAD = 128
FACTOR = HEAD**-0.5
LOG2E = 1.4426950408889634
SCALE2 = FACTOR * LOG2E
NEG_FILL = -1e30
BLOCK = 128
HEADS = 4
ROWS = HEADS * BLOCK
CHUNK = 2 * BLOCK
VMEM_LIMIT = 24 * 1024 * 1024
BF16 = jnp.bfloat16
F32 = jnp.float32


def shifted(size, step):
    return [(i, (i + step) % size) for i in range(size)]


def contract_last(left, right):
    return lax.dot_general(
        left, right, (((1,), (1,)), ((), ())), preferred_element_type=F32
    )


def matmul(left, right):
    return jnp.dot(left, right, preferred_element_type=F32)


def project_kernel(first, rank, x0, x1, g0, g1, wq, wk, wv, wo, *rest):
    if first:
        sum_ref, acc = rest
    else:
        before, kv_ref, qd_ref, acc = rest
    step = pl.program_id(0)

    def add(x_ref, g_ref, start):
        x, g = x_ref[...], g_ref[...]
        parts = (
            (0, 128, matmul(x, wk[...])),
            (128, 256, matmul(x, wv[...])),
            (256, 768, matmul(x, wq[...])),
            (768, 1280, contract_last(g, wo[...])),
        )
        for low, high, part in parts:
            if start is None:
                acc[:, low:high] = part
            else:
                acc[:, low:high] = start[:, low:high] + part

    @pl.when(step == 0)
    def _():
        add(x0, g0, None if first else before)

    @pl.when(step == 1)
    def _():
        add(x1, g1, acc)
        if first:
            sum_ref[...] = acc[...]
        else:
            kv_ref[...] = acc[:, :256].astype(BF16)
            qd_ref[...] = acc[:, 256:].astype(BF16)


def project(first, rank, offset, x0, x1, g0, g1, weights, before=None):
    wq, wk, wv, wo = weights
    whole = pl.BlockSpec((BLOCK, 1024), lambda i, r: (0, 0))

    def rows(width):
        return pl.BlockSpec((1024, width), lambda i, r: (r[0] ^ (offset + i), 0))

    in_specs = [whole] * 4 + [
        rows(512),
        rows(128),
        rows(128),
        pl.BlockSpec((512, 1024), lambda i, r: (0, r[0] ^ (offset + i))),
    ]
    operands = [x0, x1, g0, g1, wq, wk, wv, wo]
    if first:
        out_shape = [jax.ShapeDtypeStruct((BLOCK, 1280), F32)]
        out_specs = [pl.BlockSpec((BLOCK, 1280), lambda i, r: (0, 0))]
    else:
        in_specs.append(pl.BlockSpec((BLOCK, 1280), lambda i, r: (0, 0)))
        operands.append(before)
        out_shape = [
            jax.ShapeDtypeStruct((BLOCK, 256), BF16),
            jax.ShapeDtypeStruct((BLOCK, 1024), BF16),
        ]
        out_specs = [
            pl.BlockSpec((BLOCK, 256), lambda i, r: (0, 0)),
            pl.BlockSpec((BLOCK, 1024), lambda i, r: (0, 0)),
        ]
    return pl.pallas_call(
        functools.partial(project_kernel, first),
        grid_spec=pltpu.PrefetchScalarGridSpec(
            num_scalar_prefetch=1,
            grid=(2,),
            in_specs=in_specs,
            out_specs=out_specs,
            scratch_shapes=[pltpu.VMEM((BLOCK, 1280), F32)],
        ),
        out_shape=out_shape,
        compiler_params=pltpu.CompilerParams(vmem_limit_bytes=VMEM_LIMIT),
        cost_estimate=pl.CostEstimate(
            flops=2 * 128 * 2048 * 1280, bytes_accessed=6 << 20, transcendentals=0
        ),
    )(rank, *operands)


def stack_heads(ref, first):
    return jnp.concatenate(
        [ref[:, first + h * HEAD : first + (h + 1) * HEAD] for h in range(HEADS)], axis=0
    )


def visible_tile(times, key_block, query_block):
    key_row = jnp.broadcast_to(times[pl.ds(key_block, 1), :], (BLOCK, BLOCK))
    seen = key_row.T <= times[pl.ds(query_block, 1), :]
    return jnp.concatenate([seen] * HEADS, axis=1)


def for_chunks(place, query_y, full, masked):
    z, y, xh = place[0], place[1], place[2]
    lax.fori_loop(0, z, lambda i, carry: (full(i), carry)[1], 0)
    masked(z)

    @pl.when((z < 7) & (y == 0) & (xh == 1) & (query_y == 3))
    def _():
        masked(z + 1)


def chunk_mask(times, place, chunk, query_y):
    z, y, xh = place[0], place[1], place[2]
    query_block = 8 * z + 2 * query_y + xh
    return jnp.concatenate(
        [visible_tile(times, 8 * chunk + 2 * y + h, query_block) for h in range(2)], axis=0
    )


def stats_kernel(place, times, kv, qd0, qd1, qd2, qd3, out, q_rows, g_rows):
    for s, qd in enumerate((qd0, qd1, qd2, qd3)):
        query_y = (place[1] - s + 4) % 4
        q_rows[...] = stack_heads(qd, 0)
        g_rows[...] = stack_heads(qd, 512)
        base = 4 * s
        out[base : base + 1, :] = jnp.full((1, ROWS), NEG_FILL, F32)
        out[base + 1 : base + 4, :] = jnp.zeros((3, ROWS), F32)

        def chunk_stats(chunk, with_mask):
            first = pl.multiple_of(chunk * CHUNK, CHUNK)
            keys = kv[pl.ds(first, CHUNK), :HEAD]
            values = kv[pl.ds(first, CHUNK), HEAD:]
            scores = contract_last(keys, q_rows[...]) * SCALE2
            if with_mask:
                seen = chunk_mask(times, place, chunk, query_y)
                scores = jnp.where(seen, scores, NEG_FILL)
            old = out[base : base + 1, :]
            top = jnp.maximum(old, jnp.max(scores, axis=0, keepdims=True))
            prob = jnp.exp2(scores - top)
            if with_mask:
                prob = jnp.where(seen, prob, 0.0)
            prob_grad = contract_last(values, g_rows[...])
            shrink = jnp.exp2(old - top)
            out[base : base + 1, :] = top
            out[base + 1 : base + 2, :] = out[base + 1 : base + 2, :] * shrink + jnp.sum(
                prob, axis=0, keepdims=True
            )
            out[base + 2 : base + 3, :] = out[base + 2 : base + 3, :] * shrink + jnp.sum(
                prob * prob_grad, axis=0, keepdims=True
            )

        for_chunks(
            place,
            query_y,
            functools.partial(chunk_stats, with_mask=False),
            functools.partial(chunk_stats, with_mask=True),
        )


def whole_specs(count):
    return [pl.BlockSpec(memory_space=pltpu.SMEM)] + [
        pl.BlockSpec(memory_space=pltpu.VMEM) for _ in range(count - 1)
    ]


def stats(place, times, kv, blocks):
    return pl.pallas_call(
        stats_kernel,
        in_specs=whole_specs(7),
        out_specs=pl.BlockSpec(memory_space=pltpu.VMEM),
        out_shape=jax.ShapeDtypeStruct((16, ROWS), F32),
        scratch_shapes=[pltpu.VMEM((ROWS, HEAD), BF16), pltpu.VMEM((ROWS, HEAD), BF16)],
        compiler_params=pltpu.CompilerParams(vmem_limit_bytes=VMEM_LIMIT),
        cost_estimate=pl.CostEstimate(
            flops=4 * 2048 * 2048 * 128, bytes_accessed=2 << 20, transcendentals=2048 * 2048
        ),
    )(place, times, kv, *blocks)


def grads_kernel(
    place, times, kv, qd0, qd1, qd2, qd3, st0, st1, st2, st3,
    dkv, dq0, dq1, dq2, dq3, sums, q_rows, g_rows, q_sum,
):
    sums[...] = jnp.zeros_like(sums)
    gathered = (st0, st1, st2, st3)
    for s, (qd, dq) in enumerate(zip((qd0, qd1, qd2, qd3), (dq0, dq1, dq2, dq3))):
        query_y = (place[1] - s + 4) % 4
        q_rows[...] = stack_heads(qd, 0)
        g_rows[...] = stack_heads(qd, 512)
        q_sum[...] = jnp.zeros_like(q_sum)
        tops, norms, dots = [], [], []
        for k, st in enumerate(gathered):
            base = 4 * ((s - k) % 4)
            tops.append(st[base : base + 1, :])
            norms.append(st[base + 1 : base + 2, :])
            dots.append(st[base + 2 : base + 3, :])
        top = functools.reduce(jnp.maximum, tops)
        scales = [jnp.exp2(t - top) for t in tops]
        norm = sum(n * f for n, f in zip(norms, scales))
        delta = sum(d * f for d, f in zip(dots, scales)) / norm
        lse = top + jnp.log2(norm)

        def chunk_grads(chunk, with_mask):
            first = pl.multiple_of(chunk * CHUNK, CHUNK)
            keys = kv[pl.ds(first, CHUNK), :HEAD]
            values = kv[pl.ds(first, CHUNK), HEAD:]
            q, g = q_rows[...], g_rows[...]
            prob = jnp.exp2(contract_last(keys, q) * SCALE2 - lse)
            if with_mask:
                prob = jnp.where(chunk_mask(times, place, chunk, query_y), prob, 0.0)
            prob_grad = contract_last(values, g)
            score_grad = (prob * (prob_grad - delta)).astype(BF16)
            sums[pl.ds(first, CHUNK), :HEAD] += matmul(score_grad, q)
            sums[pl.ds(first, CHUNK), HEAD:] += matmul(prob.astype(BF16), g)
            q_sum[...] += lax.dot_general(
                keys, score_grad, (((0,), (0,)), ((), ())), preferred_element_type=F32
            )

        for_chunks(
            place,
            query_y,
            functools.partial(chunk_grads, with_mask=False),
            functools.partial(chunk_grads, with_mask=True),
        )
        for h in range(HEADS):
            cols = slice(h * HEAD, (h + 1) * HEAD)
            dq[:, cols] = (q_sum[:, cols].T * FACTOR).astype(BF16)
    dkv[...] = sums[...].astype(BF16)


def grads(place, times, kv, blocks, gathered):
    return pl.pallas_call(
        grads_kernel,
        in_specs=whole_specs(11),
        out_specs=[pl.BlockSpec(memory_space=pltpu.VMEM)] * 5,
        out_shape=[jax.ShapeDtypeStruct((16 * BLOCK, 2 * HEAD), BF16)]
        + [jax.ShapeDtypeStruct((BLOCK, ROWS), BF16)] * 4,
        scratch_shapes=[
            pltpu.VMEM((16 * BLOCK, 2 * HEAD), F32),
            pltpu.VMEM((ROWS, HEAD), BF16),
            pltpu.VMEM((ROWS, HEAD), BF16),
            pltpu.VMEM((HEAD, ROWS), F32),
        ],
        compiler_params=pltpu.CompilerParams(vmem_limit_bytes=VMEM_LIMIT),
        cost_estimate=pl.CostEstimate(
            flops=10 * 2048 * 2048 * 128, bytes_accessed=4 << 20, transcendentals=2048 * 2048
        ),
    )(place, times, kv, *blocks, *gathered)


def back_kernel(rank, dq, dkv, wq, wk, wv, out):
    out[...] = (
        contract_last(dq[...], wq[...])
        + contract_last(dkv[:, :HEAD], wk[...])
        + contract_last(dkv[:, HEAD:], wv[...])
    ).astype(BF16)


def back(rank, first, dq, dkv, weights):
    wq, wk, wv = weights

    def rows(width):
        return pl.BlockSpec((1024, width), lambda i, r: (r[0] ^ (first - i), 0))

    return pl.pallas_call(
        back_kernel,
        grid_spec=pltpu.PrefetchScalarGridSpec(
            num_scalar_prefetch=1,
            grid=(2,),
            in_specs=[
                pl.BlockSpec((BLOCK, 512), lambda i, r: (0, 0)),
                pl.BlockSpec((BLOCK, 256), lambda i, r: (0, 0)),
                rows(512),
                rows(128),
                rows(128),
            ],
            out_specs=pl.BlockSpec((None, BLOCK, 1024), lambda i, r: (i, 0, 0)),
        ),
        out_shape=jax.ShapeDtypeStruct((2, BLOCK, 1024), BF16),
        compiler_params=pltpu.CompilerParams(vmem_limit_bytes=VMEM_LIMIT),
        cost_estimate=pl.CostEstimate(
            flops=2 * 128 * 2048 * 768, bytes_accessed=4 << 20, transcendentals=0
        ),
    )(rank, dq, dkv, wq, wk, wv)


def local(inputs, out_grad, w_query, key_weight, value_weight, w_output, times):
    z, y, xh = lax.axis_index("z"), lax.axis_index("y"), lax.axis_index("xh")
    xl, core = lax.axis_index("xl"), lax.axis_index("core")
    rank = (2 * xl + core).astype(jnp.int32).reshape(1)
    place = jnp.stack([z, y, xh]).astype(jnp.int32)
    times2d = times.reshape(64, BLOCK)
    swap = shifted(2, 1)

    def to_core(value):
        return lax.ppermute(value, "core", swap)

    def to_xl(value):
        return lax.ppermute(value, "xl", swap)

    x2, g2 = to_xl(inputs), to_xl(out_grad)
    x1, g1 = to_core(inputs), to_core(out_grad)
    weights = (w_query, key_weight, value_weight, w_output)
    (half,) = project(True, rank, 0, inputs, x1, out_grad, g1, weights)
    x3, g3 = to_core(x2), to_core(g2)
    kv_own, qd_own = project(False, rank, 2, x2, x3, g2, g3, weights, half)

    blocks = [qd_own] + [lax.ppermute(qd_own, "y", shifted(4, s)) for s in (1, 2, 3)]
    kv = lax.all_to_all(
        jnp.broadcast_to(kv_own, (16,) + kv_own.shape), ("z", "xh"), 0, 0, tiled=True
    ).reshape(16 * BLOCK, 2 * HEAD)

    own_stats = stats(place, times2d, kv, blocks)
    gathered = [own_stats] + [lax.ppermute(own_stats, "y", shifted(4, s)) for s in (1, 2, 3)]
    dkv, *dqs = grads(place, times2d, kv, blocks, gathered)

    dq_parts = [dqs[0]] + [lax.ppermute(dqs[s], "y", shifted(4, -s)) for s in (1, 2, 3)]
    dkv_parts = lax.all_to_all(
        dkv.reshape(16, BLOCK, 2 * HEAD), ("z", "xh"), 0, 0, tiled=True
    )
    dq = sum(part.astype(F32) for part in dq_parts).astype(BF16)
    dkv_sum = jnp.sum(dkv_parts.astype(F32), axis=0)
    dk = (dkv_sum[:, :HEAD] * FACTOR).astype(BF16)
    dv = dkv_sum[:, HEAD:].astype(BF16)
    dkv_own = jnp.concatenate([dk, dv], axis=1)

    back_weights = (w_query, key_weight, value_weight)
    far = back(rank, 3, dq, dkv_own, back_weights)
    far_sum = (far[1].astype(F32) + to_core(far[0]).astype(F32)).astype(BF16)
    from_far = to_xl(far_sum)
    near = back(rank, 1, dq, dkv_own, back_weights)
    input_grad = (
        near[1].astype(F32) + to_core(near[0]).astype(F32) + from_far.astype(F32)
    ).astype(BF16)
    return input_grad, dk, dv


def solution(mesh):
    split = Mesh(mesh.devices.reshape(8, 4, 2, 2, 2), ("z", "y", "xh", "xl", "core"))
    ctx, tp = ("z", "y", "xh"), ("xl", "core")
    in_specs = (
        P(ctx, tp),
        P(ctx, tp),
        P(None, tp),
        P(None, tp),
        P(None, tp),
        P(tp, None),
        P(),
    )
    out_specs = (P(ctx, tp), P(ctx, tp), P(ctx, tp))
    return jax.shard_map(
        local, mesh=split, in_specs=in_specs, out_specs=out_specs, check_vma=False
    )
```

```python
import functools

import jax
import jax.numpy as jnp
from jax import lax
from jax.experimental import pallas as pl
from jax.experimental.pallas import tpu as pltpu
from jax.sharding import Mesh
from jax.sharding import PartitionSpec as P

HEAD = 128
FACTOR = HEAD**-0.5
LOG2E = 1.4426950408889634
SCALE2 = FACTOR * LOG2E
NEG_FILL = -1e30
BLOCK = 128
HEADS = 4
ROWS = HEADS * BLOCK
CHUNK = 2 * BLOCK
FAR_FLOPS = 15_000_000_000
PARTS = 4
PART = 2048 // PARTS
STEP = 512
VMEM_LIMIT = 20 * 1024 * 1024
BF16 = jnp.bfloat16
F32 = jnp.float32


def shifted(size, step):
    return [(i, (i + step) % size) for i in range(size)]


def contract_last(left, right):
    return lax.dot_general(
        left, right, (((1,), (1,)), ((), ())), preferred_element_type=F32
    )


def matmul(left, right):
    return jnp.dot(left, right, preferred_element_type=F32)


PAIR = 2048


def near_kernel(
    place, x0, x1, g0, g1, wq, wk, wv, wo,
    x_half, g_half, far_q, far_k, far_v, far_o,
    near_q, near_k, near_v, near_o, g_buf, sems,
):
    xl, core = place[3], place[4]
    near = pl.ds(pl.multiple_of(xl * PAIR, PAIR), PAIR)
    far = pl.ds(pl.multiple_of((1 - xl) * PAIR, PAIR), PAIR)
    copies = []
    for rows, targets in (
        (near, (near_q, near_k, near_v, near_o)),
        (far, (far_q, far_k, far_v, far_o)),
    ):
        for source, target in zip((wq, wk, wv, wo), targets):
            part = source.at[:, rows] if source is wo else source.at[rows, :]
            copies.append(pltpu.make_async_copy(part, target, sems.at[len(copies)]))
    for copy in copies:
        copy.start()
    own, other = core_halves(core)
    for copy, weight, low, high in (
        (copies[0], near_q, 256, 768),
        (copies[1], near_k, 0, 128),
        (copies[2], near_v, 128, 256),
    ):
        copy.wait()
        x_half[:, low:high] = matmul(x0[...], weight[own, :]) + matmul(x1[...], weight[other, :])
    copies[3].wait()
    g_buf[...] = contract_last(g0[...], near_o[:, own]) + contract_last(g1[...], near_o[:, other])
    copies.append(pltpu.make_async_copy(g_buf, g_half, sems.at[8]))
    copies[8].start()
    for copy in copies[4:]:
        copy.wait()


def core_halves(core):
    return [pl.ds(pl.multiple_of(c * 1024, 1024), 1024) for c in (core, 1 - core)]


def far_inputs_kernel(place, x2, x3, wq, wk, wv, x_half, kv, q, kv_buf, q_buf, sems):
    own, other = core_halves(place[4])

    def product(weight, low, high):
        return (
            x_half[:, low:high]
            + matmul(x2[...], weight[own, :])
            + matmul(x3[...], weight[other, :])
        ).astype(BF16)

    kv_buf[:, :HEAD] = product(wk, 0, 128)
    kv_buf[:, HEAD:] = product(wv, 128, 256)
    copies = [pltpu.make_async_copy(kv_buf, kv.at[i], sems.at[i]) for i in range(16)]
    for copy in copies:
        copy.start()
    q_buf[...] = product(wq, 256, 768)
    copies.append(pltpu.make_async_copy(q_buf, q, sems.at[16]))
    copies[16].start()
    for copy in copies:
        copy.wait()


def far_grads_kernel(place, g2, g3, wo, g_half, q, out, g_buf, out_buf, sems):
    own, other = core_halves(place[4])
    fetch_g = pltpu.make_async_copy(g_half, g_buf, sems.at[0])
    fetch_q = pltpu.make_async_copy(q, out_buf.at[:, :ROWS], sems.at[1])
    fetch_g.start()
    fetch_q.start()
    far = contract_last(g2[...], wo[:, own]) + contract_last(g3[...], wo[:, other])
    fetch_g.wait()
    out_buf[:, ROWS:] = (g_buf[...] + far).astype(BF16)
    fetch_q.wait()
    store = pltpu.make_async_copy(out_buf, out, sems.at[2])
    store.start()
    store.wait()


def whole_call(
    kernel, operands, outs, scratch=(), hbm=(), hbm_outs=(), flops=0, traffic=0, exps=0
):
    vmem = pl.BlockSpec(memory_space=pltpu.VMEM)
    operands = list(operands)
    in_specs = [vmem] * len(operands)
    in_specs[0] = pl.BlockSpec(memory_space=pltpu.SMEM)
    for i in hbm:
        in_specs[i] = pl.BlockSpec(memory_space=pltpu.HBM)
        operands[i] = pltpu.with_memory_space_constraint(operands[i], pltpu.HBM)
    return pl.pallas_call(
        kernel,
        in_specs=in_specs,
        out_specs=[
            pl.BlockSpec(memory_space=pltpu.HBM) if i in hbm_outs else vmem
            for i in range(len(outs))
        ],
        out_shape=outs,
        scratch_shapes=list(scratch),
        compiler_params=pltpu.CompilerParams(vmem_limit_bytes=VMEM_LIMIT),
        cost_estimate=pl.CostEstimate(flops=flops, bytes_accessed=traffic, transcendentals=exps),
    )(*operands)


def stack_heads(ref, first):
    return jnp.concatenate(
        [ref[:, first + h * HEAD : first + (h + 1) * HEAD] for h in range(HEADS)], axis=0
    )


def visible_tile(times, key_block, query_block):
    key_row = jnp.broadcast_to(times[pl.ds(key_block, 1), :], (BLOCK, BLOCK))
    seen = key_row.T <= times[pl.ds(query_block, 1), :]
    return jnp.concatenate([seen] * HEADS, axis=1)


def for_tiles(place, times, tile):
    z, y, xh = place[0], place[1], place[2]

    def past(first, keys):
        for part in range(PARTS):
            tile(pl.multiple_of(first, CHUNK), keys, part * PART, PART, None)

    def some(i, carry):
        past(i * STEP, STEP)
        return carry

    lax.fori_loop(0, z * CHUNK // STEP, some, 0)
    if STEP > CHUNK:

        @pl.when(z % 2 == 1)
        def _():
            past((z - 1) * CHUNK, CHUNK)

    for s in range(4):
        query_block = 8 * z + 2 * ((y - s + 4) % 4) + xh
        mask = jnp.concatenate(
            [visible_tile(times, 8 * z + 2 * y + h, query_block) for h in range(2)], axis=0
        )
        tile(pl.multiple_of(z * CHUNK, CHUNK), CHUNK, s * ROWS, ROWS, mask)

    @pl.when((z < 7) & (y == 0) & (xh == 1))
    def _():
        mask = visible_tile(times, 8 * (z + 1), 8 * z + 7)
        tile(pl.multiple_of((z + 1) * CHUNK, CHUNK), BLOCK, ROWS, ROWS, mask)


def fetch(times, own, times_buf, own_buf, sems):
    copies = [
        pltpu.make_async_copy(own, own_buf, sems.at[0]),
        pltpu.make_async_copy(times, times_buf, sems.at[1]),
    ]
    for copy in copies:
        copy.start()
    return copies


FETCHED = [
    pltpu.VMEM((64, BLOCK), jnp.int32),
    pltpu.VMEM((BLOCK, 1024), BF16),
    pltpu.SemaphoreType.DMA((2,)),
]


def stack_blocks(blocks, copies, q_rows, g_rows):
    for s in (1, 2, 3, 0):
        if s == 0:
            for copy in copies:
                copy.wait()
        q_rows[s * ROWS : (s + 1) * ROWS, :] = stack_heads(blocks[s], 0)
        g_rows[s * ROWS : (s + 1) * ROWS, :] = stack_heads(blocks[s], 512)


def stats_kernel(
    place, times_hbm, kv, qd0, qd1, qd2, qd3, out, times, own, sems, q_rows, g_rows
):
    copies = fetch(times_hbm, qd0, times, own, sems)
    stack_blocks((own, qd1, qd2, qd3), copies, q_rows, g_rows)
    out[0:1, :] = jnp.full((1, 4 * ROWS), NEG_FILL, F32)
    out[1:4, :] = jnp.zeros((3, 4 * ROWS), F32)

    def tile(first, count, row, rows, seen):
        cols = slice(row, row + rows)
        keys = kv[pl.ds(first, count), :HEAD]
        values = kv[pl.ds(first, count), HEAD:]
        scores = contract_last(keys, q_rows[cols, :]) * SCALE2
        if seen is not None:
            scores = jnp.where(seen, scores, NEG_FILL)
        old = out[0:1, cols]
        top = jnp.maximum(old, jnp.max(scores, axis=0, keepdims=True))
        prob = jnp.exp2(scores - top)
        if seen is not None:
            prob = jnp.where(seen, prob, 0.0)
        prob_grad = contract_last(values, g_rows[cols, :])
        shrink = jnp.exp2(old - top)
        out[0:1, cols] = top
        out[1:2, cols] = out[1:2, cols] * shrink + jnp.sum(prob, axis=0, keepdims=True)
        out[2:3, cols] = out[2:3, cols] * shrink + jnp.sum(
            prob * prob_grad, axis=0, keepdims=True
        )

    for_tiles(place, times, tile)


def stats(place, times, kv, blocks):
    (out,) = whole_call(
        stats_kernel,
        (place, times, kv, *blocks),
        [jax.ShapeDtypeStruct((4, 4 * ROWS), F32)],
        FETCHED + [pltpu.VMEM((4 * ROWS, HEAD), BF16)] * 2,
        hbm=(1, 3),
        flops=4 * 2048 * 2048 * 128,
        traffic=2 << 20,
        exps=2048 * 2048,
    )
    return out


def grads_kernel(
    place, times_hbm, kv, qd0, qd1, qd2, qd3, st0, st1, st2, st3,
    dkv, dq0, dq1, dq2, dq3,
    times, own, sems, sums, q_rows, g_rows, q_sum, row_stats, dkv_buf, dq_buf, out_sems,
):
    copies = fetch(times_hbm, qd0, times, own, sems)
    sums[...] = jnp.zeros_like(sums)
    q_sum[...] = jnp.zeros_like(q_sum)
    for s in range(4):
        cols = slice(s * ROWS, (s + 1) * ROWS)
        tops, norms, dots = [], [], []
        for k, st in enumerate((st0, st1, st2, st3)):
            first = ((s - k) % 4) * ROWS
            tops.append(st[0:1, first : first + ROWS])
            norms.append(st[1:2, first : first + ROWS])
            dots.append(st[2:3, first : first + ROWS])
        top = functools.reduce(jnp.maximum, tops)
        scales = [jnp.exp2(t - top) for t in tops]
        norm = sum(n * f for n, f in zip(norms, scales))
        row_stats[0:1, cols] = top + jnp.log2(norm)
        row_stats[1:2, cols] = sum(d * f for d, f in zip(dots, scales)) / norm
    stack_blocks((own, qd1, qd2, qd3), copies, q_rows, g_rows)

    def tile(first, count, row, rows, seen):
        cols = slice(row, row + rows)
        keys = kv[pl.ds(first, count), :HEAD]
        values = kv[pl.ds(first, count), HEAD:]
        q, g = q_rows[cols, :], g_rows[cols, :]
        prob = jnp.exp2(contract_last(keys, q) * SCALE2 - row_stats[0:1, cols])
        if seen is not None:
            prob = jnp.where(seen, prob, 0.0)
        prob_grad = contract_last(values, g)
        score_grad = (prob * (prob_grad - row_stats[1:2, cols])).astype(BF16)
        sums[pl.ds(first, count), :HEAD] += matmul(score_grad, q)
        sums[pl.ds(first, count), HEAD:] += matmul(prob.astype(BF16), g)
        q_sum[:, cols] += lax.dot_general(
            keys, score_grad, (((0,), (0,)), ((), ())), preferred_element_type=F32
        )

    for_tiles(place, times, tile)
    outs = []
    for i in range(16):
        dkv_buf[i] = sums[i * BLOCK : (i + 1) * BLOCK, :].astype(BF16)
        if i % 4 == 3:
            part = pl.ds(i - 3, 4)
            outs.append(
                pltpu.make_async_copy(dkv_buf.at[part], dkv.at[part], out_sems.at[i // 4])
            )
            outs[-1].start()
    for s, dq in enumerate((dq0, dq1, dq2, dq3)):
        for h in range(HEADS):
            part = q_sum[:, s * ROWS + h * HEAD : s * ROWS + (h + 1) * HEAD]
            dq_buf[s, :, h * HEAD : (h + 1) * HEAD] = (part.T * FACTOR).astype(BF16)
        outs.append(pltpu.make_async_copy(dq_buf.at[s], dq, out_sems.at[4 + s]))
        outs[-1].start()
    for copy in outs:
        copy.wait()


def grads(place, times, kv, blocks, gathered):
    return whole_call(
        grads_kernel,
        (place, times, kv, *blocks, *gathered),
        [jax.ShapeDtypeStruct((16, BLOCK, 2 * HEAD), BF16)]
        + [jax.ShapeDtypeStruct((BLOCK, ROWS), BF16)] * 4,
        FETCHED
        + [
            pltpu.VMEM((16 * BLOCK, 2 * HEAD), F32),
            pltpu.VMEM((4 * ROWS, HEAD), BF16),
            pltpu.VMEM((4 * ROWS, HEAD), BF16),
            pltpu.VMEM((HEAD, 4 * ROWS), F32),
            pltpu.VMEM((8, 4 * ROWS), F32),
            pltpu.VMEM((16, BLOCK, 2 * HEAD), BF16),
            pltpu.VMEM((4, BLOCK, ROWS), BF16),
            pltpu.SemaphoreType.DMA((8,)),
        ],
        hbm=(1, 3),
        hbm_outs=(0, 1, 2, 3, 4),
        flops=10 * 2048 * 2048 * 128,
        traffic=4 << 20,
        exps=2048 * 2048,
    )


def feature_rows(place, flip):
    first = (2 * place[3] + place[4]) ^ flip
    return pl.ds(pl.multiple_of(first * 1024, 1024), 1024)


def query_back_kernel(
    place, dq0, dq1, dq2, dq3, wq, wk, wv, far0, far1, near1, near0, out_k, out_v, held, sems
):
    copies = [
        pltpu.make_async_copy(wq.at[feature_rows(place, flip), :], held.at[i], sems.at[i])
        for i, flip in enumerate((3, 2, 1, 0))
    ]
    copies.append(pltpu.make_async_copy(wk, out_k, sems.at[4]))
    copies.append(pltpu.make_async_copy(wv, out_v, sems.at[5]))
    for copy in copies:
        copy.start()
    parts = [d[...].astype(F32) for d in (dq0, dq1, dq2, dq3)]
    total = (parts[0] + parts[1] + parts[2] + parts[3]).astype(BF16)
    for i, out in enumerate((far0, far1, near1, near0)):
        copies[i].wait()
        out[...] = contract_last(total, held[i]).astype(out.dtype)
    copies[4].wait()
    copies[5].wait()


def key_terms(place, flip, dk, dv, wk, wv):
    rows = feature_rows(place, flip)
    return contract_last(dk, wk[rows, :]) + contract_last(dv, wv[rows, :])


def key_far_kernel(place, parts, wk, wv, queries, far0, far1, dk, dv, dkv):
    total = parts[0].astype(F32)
    for i in range(1, 16):
        total = total + parts[i].astype(F32)
    dk[...] = (total[:, :HEAD] * FACTOR).astype(BF16)
    dv[...] = total[:, HEAD:].astype(BF16)
    dkv[:, :HEAD] = dk[...]
    dkv[:, HEAD:] = dv[...]
    far0[...] = key_terms(place, 3, dk[...], dv[...], wk, wv).astype(BF16)
    far1[...] = queries[...].astype(F32) + key_terms(place, 2, dk[...], dv[...], wk, wv)


def key_near_kernel(place, dkv, wk, wv, queries, near1, near0):
    dk, dv = dkv[:, :HEAD], dkv[:, HEAD:]
    near1[...] = key_terms(place, 1, dk, dv, wk, wv).astype(BF16)
    near0[...] = queries[...].astype(F32) + key_terms(place, 0, dk, dv, wk, wv)


def local(inputs, out_grad, w_query, key_weight, value_weight, w_output, times):
    axes = ("z", "y", "xh", "xl", "core")
    place = jnp.stack([lax.axis_index(name) for name in axes]).astype(jnp.int32)
    times2d = times.reshape(64, BLOCK)
    swap = shifted(2, 1)

    def to_core(value):
        return lax.ppermute(value, "core", swap)

    def to_xl(value):
        return lax.ppermute(value, "xl", swap)

    def shape(*dims, kind=BF16):
        return jax.ShapeDtypeStruct(dims, kind)

    x2, g2 = to_xl(inputs), to_xl(out_grad)
    x1, g1 = to_core(inputs), to_core(out_grad)
    held = [
        shape(PAIR, ROWS), shape(PAIR, HEAD), shape(PAIR, HEAD), shape(ROWS, PAIR)
    ]
    x_half, g_half, far_q, far_k, far_v, far_o = whole_call(
        near_kernel,
        (place, inputs, x1, out_grad, g1, w_query, key_weight, value_weight, w_output),
        [shape(BLOCK, 768, kind=F32), shape(BLOCK, ROWS, kind=F32)] + held,
        [pltpu.VMEM(h.shape, BF16) for h in held]
        + [pltpu.VMEM((BLOCK, ROWS), F32), pltpu.SemaphoreType.DMA((9,))],
        hbm=(5, 6, 7, 8),
        hbm_outs=(1,),
        flops=2 * 128 * 2048 * 1280,
        traffic=10 << 20,
    )
    x2, x_half, g_half = lax.optimization_barrier((x2, x_half, g_half))
    x3 = to_core(x2)
    kv_own, q_own = whole_call(
        far_inputs_kernel,
        (place, x2, x3, far_q, far_k, far_v, x_half),
        [shape(16, BLOCK, 2 * HEAD), shape(BLOCK, ROWS)],
        [
            pltpu.VMEM((BLOCK, 2 * HEAD), BF16),
            pltpu.VMEM((BLOCK, ROWS), BF16),
            pltpu.SemaphoreType.DMA((17,)),
        ],
        hbm_outs=(0, 1),
        flops=2 * 128 * 2048 * 768,
        traffic=4 << 20,
    )
    g2, q_own = lax.optimization_barrier((g2, q_own))
    g3 = to_core(g2)
    (qd_own,) = whole_call(
        far_grads_kernel,
        (place, g2, g3, far_o, g_half, q_own),
        [shape(BLOCK, 1024)],
        [
            pltpu.VMEM((BLOCK, ROWS), F32),
            pltpu.VMEM((BLOCK, 1024), BF16),
            pltpu.SemaphoreType.DMA((3,)),
        ],
        hbm=(4, 5),
        hbm_outs=(0,),
        flops=FAR_FLOPS,
        traffic=3 << 20,
    )
    kv = lax.all_to_all(kv_own, ("z", "xh"), 0, 0, tiled=True).reshape(16 * BLOCK, 2 * HEAD)
    blocks = [qd_own] + [lax.ppermute(qd_own, "y", shifted(4, s)) for s in (1, 2, 3)]

    own_stats = stats(place, times2d, kv, blocks)
    gathered = [own_stats] + [lax.ppermute(own_stats, "y", shifted(4, s)) for s in (1, 2, 3)]
    dkv, *dqs = grads(place, times2d, kv, blocks, gathered)

    dkv_parts = lax.all_to_all(dkv, ("z", "xh"), 0, 0, tiled=True)
    dq_parts = [dqs[0]] + [lax.ppermute(dqs[s], "y", shifted(4, -s)) for s in (1, 2, 3)]

    def add(*values):
        return sum(v.astype(F32) for v in values)

    far0, far1, near1, near0, held_k, held_v = whole_call(
        query_back_kernel,
        (place, *dq_parts, w_query, key_weight, value_weight),
        [shape(BLOCK, 1024)] * 4 + [shape(2 * PAIR, HEAD)] * 2,
        [pltpu.VMEM((4, 1024, ROWS), BF16), pltpu.SemaphoreType.DMA((6,))],
        hbm=(5, 6, 7),
        flops=2 * 128 * 4096 * 512,
        traffic=8 << 20,
    )
    far_query = add(far1, to_core(far0)).astype(BF16)
    near_query = add(near0, to_core(near1)).astype(BF16)

    far0, far1, dk, dv, dkv_own = whole_call(
        key_far_kernel,
        (place, dkv_parts, held_k, held_v, far_query),
        [shape(BLOCK, 1024), shape(BLOCK, 1024, kind=F32)]
        + [shape(BLOCK, HEAD)] * 2
        + [shape(BLOCK, 2 * HEAD)],
        flops=2 * 128 * 2048 * 256,
        traffic=2 << 20,
    )
    far_sum, dkv_own = lax.optimization_barrier(
        (add(far1, to_core(far0)).astype(BF16), dkv_own)
    )
    from_far = to_xl(far_sum)
    near1, near0 = whole_call(
        key_near_kernel,
        (place, dkv_own, held_k, held_v, near_query),
        [shape(BLOCK, 1024), shape(BLOCK, 1024, kind=F32)],
        flops=2 * 128 * 2048 * 256,
        traffic=2 << 20,
    )
    input_grad = add(near0, to_core(near1), from_far).astype(BF16)
    return input_grad, dk, dv


def solution(mesh):
    split = Mesh(mesh.devices.reshape(8, 4, 2, 2, 2), ("z", "y", "xh", "xl", "core"))
    ctx, tp = ("z", "y", "xh"), ("xl", "core")
    in_specs = (
        P(ctx, tp),
        P(ctx, tp),
        P(None, tp),
        P(None, tp),
        P(None, tp),
        P(tp, None),
        P(),
    )
    out_specs = (P(ctx, tp), P(ctx, tp), P(ctx, tp))
    return jax.shard_map(
        local, mesh=split, in_specs=in_specs, out_specs=out_specs, check_vma=False
    )
```

```python
import functools

import jax
import jax.numpy as jnp
from jax import lax
from jax.experimental import pallas as pl
from jax.experimental.pallas import tpu as pltpu
from jax.sharding import Mesh
from jax.sharding import PartitionSpec as P

HEAD = 128
FACTOR = HEAD**-0.5
LOG2E = 1.4426950408889634
SCALE2 = FACTOR * LOG2E
NEG_FILL = -1e30
LOWEST_TOP = -1e29
BLOCK = 128
HEADS = 4
ROWS = HEADS * BLOCK
CHUNK = 2 * BLOCK
FAR_FLOPS = 15_000_000_000
STEP = 512
VMEM_LIMIT = 20 * 1024 * 1024
BF16 = jnp.bfloat16
F32 = jnp.float32


def shifted(size, step):
    return [(i, (i + step) % size) for i in range(size)]


def contract_last(left, right):
    return lax.dot_general(
        left, right, (((1,), (1,)), ((), ())), preferred_element_type=F32
    )


def matmul(left, right):
    return jnp.dot(left, right, preferred_element_type=F32)


PAIR = 2048


def near_kernel(
    place, x0, x1, g0, g1, wq, wk, wv, wo,
    x_half, g_half, far_q, far_k, far_v, far_o,
    near_q, near_k, near_v, near_o, g_buf, sems,
):
    xl, core = place[3], place[4]
    near = pl.ds(pl.multiple_of(xl * PAIR, PAIR), PAIR)
    far = pl.ds(pl.multiple_of((1 - xl) * PAIR, PAIR), PAIR)
    copies = []
    for rows, targets in (
        (near, (near_q, near_k, near_v, near_o)),
        (far, (far_q, far_k, far_v, far_o)),
    ):
        for source, target in zip((wq, wk, wv, wo), targets):
            part = source.at[:, rows] if source is wo else source.at[rows, :]
            copies.append(pltpu.make_async_copy(part, target, sems.at[len(copies)]))
    for copy in copies:
        copy.start()
    own, other = core_halves(core)
    for copy, weight, low, high in (
        (copies[0], near_q, 256, 768),
        (copies[1], near_k, 0, 128),
        (copies[2], near_v, 128, 256),
    ):
        copy.wait()
        x_half[:, low:high] = matmul(x0[...], weight[own, :]) + matmul(x1[...], weight[other, :])
    copies[3].wait()
    g_buf[...] = contract_last(g0[...], near_o[:, own]) + contract_last(g1[...], near_o[:, other])
    copies.append(pltpu.make_async_copy(g_buf, g_half, sems.at[8]))
    copies[8].start()
    for copy in copies[4:]:
        copy.wait()


def core_halves(core):
    return [pl.ds(pl.multiple_of(c * 1024, 1024), 1024) for c in (core, 1 - core)]


def far_inputs_kernel(place, x2, x3, wq, wk, wv, x_half, kv, q, kv_buf, q_buf, sems):
    own, other = core_halves(place[4])

    def product(weight, low, high):
        return (
            x_half[:, low:high]
            + matmul(x2[...], weight[own, :])
            + matmul(x3[...], weight[other, :])
        ).astype(BF16)

    kv_buf[:, :HEAD] = product(wk, 0, 128)
    kv_buf[:, HEAD:] = product(wv, 128, 256)
    copies = [pltpu.make_async_copy(kv_buf, kv.at[i], sems.at[i]) for i in range(16)]
    for copy in copies:
        copy.start()
    q_buf[...] = product(wq, 256, 768)
    copies.append(pltpu.make_async_copy(q_buf, q, sems.at[16]))
    copies[16].start()
    for copy in copies:
        copy.wait()


def far_grads_kernel(place, g2, g3, wo, g_half, q, out, g_buf, out_buf, sems):
    own, other = core_halves(place[4])
    fetch_g = pltpu.make_async_copy(g_half, g_buf, sems.at[0])
    fetch_q = pltpu.make_async_copy(q, out_buf.at[:, :ROWS], sems.at[1])
    fetch_g.start()
    fetch_q.start()
    far = contract_last(g2[...], wo[:, own]) + contract_last(g3[...], wo[:, other])
    fetch_g.wait()
    out_buf[:, ROWS:] = (g_buf[...] + far).astype(BF16)
    fetch_q.wait()
    store = pltpu.make_async_copy(out_buf, out, sems.at[2])
    store.start()
    store.wait()


def whole_call(
    kernel, operands, outs, scratch=(), hbm=(), hbm_outs=(), flops=0, traffic=0, exps=0
):
    vmem = pl.BlockSpec(memory_space=pltpu.VMEM)
    operands = list(operands)
    in_specs = [vmem] * len(operands)
    in_specs[0] = pl.BlockSpec(memory_space=pltpu.SMEM)
    for i in hbm:
        in_specs[i] = pl.BlockSpec(memory_space=pltpu.HBM)
        operands[i] = pltpu.with_memory_space_constraint(operands[i], pltpu.HBM)
    return pl.pallas_call(
        kernel,
        in_specs=in_specs,
        out_specs=[
            pl.BlockSpec(memory_space=pltpu.HBM) if i in hbm_outs else vmem
            for i in range(len(outs))
        ],
        out_shape=outs,
        scratch_shapes=list(scratch),
        compiler_params=pltpu.CompilerParams(vmem_limit_bytes=VMEM_LIMIT),
        cost_estimate=pl.CostEstimate(flops=flops, bytes_accessed=traffic, transcendentals=exps),
    )(*operands)


def stack_heads(ref, first):
    return jnp.concatenate(
        [ref[:, first + h * HEAD : first + (h + 1) * HEAD] for h in range(HEADS)], axis=0
    )


def visible(times, key_block, query_block):
    keys = jnp.broadcast_to(times[pl.ds(key_block, 1), :], (BLOCK, BLOCK)).T
    return jnp.where(keys <= times[pl.ds(query_block, 1), :], 0.0, NEG_FILL)


def stack_kernel(place, times_hbm, qd0, qd1, qd2, qd3, q_rows, g_rows, bias, times, own, sems):
    copies = [
        pltpu.make_async_copy(qd0, own, sems.at[0]),
        pltpu.make_async_copy(times_hbm, times, sems.at[1]),
    ]
    for copy in copies:
        copy.start()
    for s, qd in ((1, qd1), (2, qd2), (3, qd3), (0, own)):
        if s == 0:
            copies[0].wait()
        q_rows[s * ROWS : (s + 1) * ROWS, :] = stack_heads(qd, 0)
        g_rows[s * ROWS : (s + 1) * ROWS, :] = stack_heads(qd, 512)
    copies[1].wait()
    z, y, xh = place[0], place[1], place[2]
    for s in range(4):
        cols = slice(s * BLOCK, (s + 1) * BLOCK)
        query_block = 8 * z + 2 * ((y - s + 4) % 4) + xh
        for h in range(2):
            key_block = 8 * z + 2 * y + h
            bias[h * BLOCK : (h + 1) * BLOCK, cols] = visible(times, key_block, query_block)
    bias[2 * BLOCK :, :BLOCK] = visible(times, 8 * jnp.minimum(z + 1, 7), 8 * z + 7)
    bias[2 * BLOCK :, BLOCK:] = jnp.full((BLOCK, 3 * BLOCK), NEG_FILL, F32)


def for_tiles(place, bias, tile, done):
    z, y, xh = place[0], place[1], place[2]

    def masked(part, s):
        return jnp.concatenate([bias[part, s * BLOCK : (s + 1) * BLOCK]] * HEADS, axis=1)

    for s in range(4):
        first = pl.multiple_of(z * CHUNK, CHUNK)
        tile(first, CHUNK, s * ROWS, ROWS, masked(slice(0, CHUNK), s))

    def past(first, keys):
        tile(pl.multiple_of(first, CHUNK), keys, 0, 4 * ROWS, None)

    def some(i, carry):
        past(i * STEP, STEP)
        done(i)
        return carry

    lax.fori_loop(0, z // 2, some, 0)

    @pl.when(z % 2 == 1)
    def _():
        past((z - 1) * CHUNK, CHUNK)

    @pl.when((z < 7) & (y == 0) & (xh == 1))
    def _():
        first = pl.multiple_of((z + 1) * CHUNK, CHUNK)
        tile(first, BLOCK, ROWS, ROWS, masked(slice(CHUNK, CHUNK + BLOCK), 0))


def stats_kernel(place, kv, q_rows, g_rows, bias, out):
    def tile(first, count, row, rows, hidden):
        cols = slice(row, row + rows)
        keys = kv[pl.ds(first, count), :HEAD]
        values = kv[pl.ds(first, count), HEAD:]
        scores = contract_last(keys, q_rows[cols, :]) * SCALE2
        first_visit = hidden is not None and count == CHUNK
        if hidden is not None:
            scores = scores + hidden
        top = jnp.maximum(jnp.max(scores, axis=0, keepdims=True), LOWEST_TOP)
        if not first_visit:
            old = out[0:1, cols]
            top = jnp.maximum(old, top)
        prob = jnp.exp2(scores - top)
        prob_grad = contract_last(values, g_rows[cols, :])
        norm = jnp.sum(prob, axis=0, keepdims=True)
        dot = jnp.sum(prob * prob_grad, axis=0, keepdims=True)
        if not first_visit:
            shrink = jnp.exp2(old - top)
            norm += out[1:2, cols] * shrink
            dot += out[2:3, cols] * shrink
        out[0:1, cols] = top
        out[1:2, cols] = norm
        out[2:3, cols] = dot

    out[3:4, :] = jnp.zeros((1, 4 * ROWS), F32)
    for_tiles(place, bias, tile, lambda i: None)


def stats(place, kv, rows):
    (out,) = whole_call(
        stats_kernel,
        (place, kv, *rows),
        [jax.ShapeDtypeStruct((4, 4 * ROWS), F32)],
        flops=4 * 2048 * 2048 * 128,
        traffic=2 << 20,
        exps=2048 * 2048,
    )
    return out


def grads_kernel(
    place, kv, q_rows, g_rows, bias, st0, st1, st2, st3,
    dkv, dq0, dq1, dq2, dq3,
    sums, q_sum, row_stats, dkv_buf, dq_buf, out_sems,
):
    z = place[0]

    def clear(i, carry):
        dkv_buf[i] = jnp.zeros((BLOCK, 2 * HEAD), BF16)
        return carry

    lax.fori_loop(2 * z + 2, 16, clear, 0)
    for s in range(4):
        cols = slice(s * ROWS, (s + 1) * ROWS)
        tops, norms, dots = [], [], []
        for k, st in enumerate((st0, st1, st2, st3)):
            first = ((s - k) % 4) * ROWS
            tops.append(st[0:1, first : first + ROWS])
            norms.append(st[1:2, first : first + ROWS])
            dots.append(st[2:3, first : first + ROWS])
        top = functools.reduce(jnp.maximum, tops)
        scales = [jnp.exp2(t - top) for t in tops]
        norm = sum(n * f for n, f in zip(norms, scales))
        row_stats[0:1, cols] = top + jnp.log2(norm)
        row_stats[1:2, cols] = sum(d * f for d, f in zip(dots, scales)) / norm

    def tile(first, count, row, rows, hidden):
        cols = slice(row, row + rows)
        keys = kv[pl.ds(first, count), :HEAD]
        values = kv[pl.ds(first, count), HEAD:]
        q, g = q_rows[cols, :], g_rows[cols, :]
        scores = contract_last(keys, q) * SCALE2
        if hidden is not None:
            scores = scores + hidden
        prob = jnp.exp2(scores - row_stats[0:1, cols])
        prob_grad = contract_last(values, g)
        score_grad = (prob * (prob_grad - row_stats[1:2, cols])).astype(BF16)
        dk = matmul(score_grad, q)
        dv = matmul(prob.astype(BF16), g)
        dq = lax.dot_general(
            keys, score_grad, (((0,), (0,)), ((), ())), preferred_element_type=F32
        )
        block = first // BLOCK
        if hidden is not None and count == CHUNK:
            q_sum[:, cols] = dq
            if row:
                dk += sums[:, :HEAD]
                dv += sums[:, HEAD:]
            sums[:, :HEAD] = dk
            sums[:, HEAD:] = dv
            if row < 3 * ROWS:
                return
        else:
            q_sum[:, cols] += dq
        for i in range(count // BLOCK):
            part = slice(i * BLOCK, (i + 1) * BLOCK)
            dkv_buf[block + i, :, :HEAD] = dk[part, :].astype(BF16)
            dkv_buf[block + i, :, HEAD:] = dv[part, :].astype(BF16)

    def send(i):
        part = pl.ds(4 * i, 4)
        return pltpu.make_async_copy(dkv_buf.at[part], dkv.at[part], out_sems.at[i])

    for_tiles(place, bias, tile, lambda i: send(i).start())
    for i in range(4):

        @pl.when(i >= z // 2)
        def _():
            send(i).start()

    outs = []
    for s, dq in enumerate((dq0, dq1, dq2, dq3)):
        for h in range(HEADS):
            part = q_sum[:, s * ROWS + h * HEAD : s * ROWS + (h + 1) * HEAD]
            dq_buf[s, :, h * HEAD : (h + 1) * HEAD] = (part.T * FACTOR).astype(BF16)
        outs.append(pltpu.make_async_copy(dq_buf.at[s], dq, out_sems.at[4 + s]))
        outs[-1].start()
    for i in range(4):
        send(i).wait()
    for copy in outs:
        copy.wait()


def grads(place, kv, rows, gathered):
    return whole_call(
        grads_kernel,
        (place, kv, *rows, *gathered),
        [jax.ShapeDtypeStruct((16, BLOCK, 2 * HEAD), BF16)]
        + [jax.ShapeDtypeStruct((BLOCK, ROWS), BF16)] * 4,
        [
            pltpu.VMEM((CHUNK, 2 * HEAD), F32),
            pltpu.VMEM((HEAD, 4 * ROWS), F32),
            pltpu.VMEM((8, 4 * ROWS), F32),
            pltpu.VMEM((16, BLOCK, 2 * HEAD), BF16),
            pltpu.VMEM((4, BLOCK, ROWS), BF16),
            pltpu.SemaphoreType.DMA((8,)),
        ],
        hbm_outs=(0, 1, 2, 3, 4),
        flops=10 * 2048 * 2048 * 128,
        traffic=4 << 20,
        exps=2048 * 2048,
    )


def feature_rows(place, flip):
    first = (2 * place[3] + place[4]) ^ flip
    return pl.ds(pl.multiple_of(first * 1024, 1024), 1024)


def query_back_kernel(
    place, dq0, dq1, dq2, dq3, wq, wk, wv, far0, far1, near1, near0, out_k, out_v, held, sems
):
    copies = [
        pltpu.make_async_copy(wq.at[feature_rows(place, flip), :], held.at[i], sems.at[i])
        for i, flip in enumerate((3, 2, 1, 0))
    ]
    copies.append(pltpu.make_async_copy(wk, out_k, sems.at[4]))
    copies.append(pltpu.make_async_copy(wv, out_v, sems.at[5]))
    for copy in copies:
        copy.start()
    parts = [d[...].astype(F32) for d in (dq0, dq1, dq2, dq3)]
    total = (parts[0] + parts[1] + parts[2] + parts[3]).astype(BF16)
    for i, out in enumerate((far0, far1, near1, near0)):
        copies[i].wait()
        out[...] = contract_last(total, held[i]).astype(out.dtype)
    copies[4].wait()
    copies[5].wait()


def key_terms(place, flip, dk, dv, wk, wv):
    rows = feature_rows(place, flip)
    return contract_last(dk, wk[rows, :]) + contract_last(dv, wv[rows, :])


def key_far_kernel(place, parts, wk, wv, queries, far0, far1, dk, dv, dkv):
    total = parts[0].astype(F32)
    for i in range(1, 16):
        total = total + parts[i].astype(F32)
    dk[...] = (total[:, :HEAD] * FACTOR).astype(BF16)
    dv[...] = total[:, HEAD:].astype(BF16)
    dkv[:, :HEAD] = dk[...]
    dkv[:, HEAD:] = dv[...]
    far0[...] = key_terms(place, 3, dk[...], dv[...], wk, wv).astype(BF16)
    far1[...] = queries[...].astype(F32) + key_terms(place, 2, dk[...], dv[...], wk, wv)


def key_near_kernel(place, dkv, wk, wv, near1, near0):
    dk, dv = dkv[:, :HEAD], dkv[:, HEAD:]
    near1[...] = key_terms(place, 1, dk, dv, wk, wv).astype(BF16)
    near0[...] = key_terms(place, 0, dk, dv, wk, wv)


def local(inputs, out_grad, w_query, key_weight, value_weight, w_output, times):
    axes = ("z", "y", "xh", "xl", "core")
    place = jnp.stack([lax.axis_index(name) for name in axes]).astype(jnp.int32)
    times2d = times.reshape(64, BLOCK)
    swap = shifted(2, 1)

    def to_core(value):
        return lax.ppermute(value, "core", swap)

    def to_xl(value):
        return lax.ppermute(value, "xl", swap)

    def shape(*dims, kind=BF16):
        return jax.ShapeDtypeStruct(dims, kind)

    x2, g2 = to_xl(inputs), to_xl(out_grad)
    x1, g1 = to_core(inputs), to_core(out_grad)
    held = [
        shape(PAIR, ROWS), shape(PAIR, HEAD), shape(PAIR, HEAD), shape(ROWS, PAIR)
    ]
    x_half, g_half, far_q, far_k, far_v, far_o = whole_call(
        near_kernel,
        (place, inputs, x1, out_grad, g1, w_query, key_weight, value_weight, w_output),
        [shape(BLOCK, 768, kind=F32), shape(BLOCK, ROWS, kind=F32)] + held,
        [pltpu.VMEM(h.shape, BF16) for h in held]
        + [pltpu.VMEM((BLOCK, ROWS), F32), pltpu.SemaphoreType.DMA((9,))],
        hbm=(5, 6, 7, 8),
        hbm_outs=(1,),
        flops=2 * 128 * 2048 * 1280,
        traffic=10 << 20,
    )
    x2, x_half, g_half = lax.optimization_barrier((x2, x_half, g_half))
    x3 = to_core(x2)
    kv_own, q_own = whole_call(
        far_inputs_kernel,
        (place, x2, x3, far_q, far_k, far_v, x_half),
        [shape(16, BLOCK, 2 * HEAD), shape(BLOCK, ROWS)],
        [
            pltpu.VMEM((BLOCK, 2 * HEAD), BF16),
            pltpu.VMEM((BLOCK, ROWS), BF16),
            pltpu.SemaphoreType.DMA((17,)),
        ],
        hbm_outs=(0, 1),
        flops=2 * 128 * 2048 * 768,
        traffic=4 << 20,
    )
    g2, q_own = lax.optimization_barrier((g2, q_own))
    g3 = to_core(g2)
    (qd_own,) = whole_call(
        far_grads_kernel,
        (place, g2, g3, far_o, g_half, q_own),
        [shape(BLOCK, 1024)],
        [
            pltpu.VMEM((BLOCK, ROWS), F32),
            pltpu.VMEM((BLOCK, 1024), BF16),
            pltpu.SemaphoreType.DMA((3,)),
        ],
        hbm=(4, 5),
        hbm_outs=(0,),
        flops=FAR_FLOPS,
        traffic=3 << 20,
    )
    kv = lax.all_to_all(kv_own, ("z", "xh"), 0, 0, tiled=True).reshape(16 * BLOCK, 2 * HEAD)
    blocks = [qd_own] + [lax.ppermute(qd_own, "y", shifted(4, s)) for s in (1, 2, 3)]

    rows = whole_call(
        stack_kernel,
        (place, times2d, *blocks),
        [shape(4 * ROWS, HEAD)] * 2 + [shape(CHUNK + BLOCK, ROWS, kind=F32)],
        [
            pltpu.VMEM((64, BLOCK), jnp.int32),
            pltpu.VMEM((BLOCK, 1024), BF16),
            pltpu.SemaphoreType.DMA((2,)),
        ],
        hbm=(1, 2),
        traffic=2 << 20,
    )
    own_stats = stats(place, kv, rows)
    gathered = [own_stats] + [lax.ppermute(own_stats, "y", shifted(4, s)) for s in (1, 2, 3)]
    dkv, *dqs = grads(place, kv, rows, gathered)

    dkv_parts = lax.all_to_all(dkv, ("z", "xh"), 0, 0, tiled=True)
    dq_parts = [dqs[0]] + [lax.ppermute(dqs[s], "y", shifted(4, -s)) for s in (1, 2, 3)]

    def add(*values):
        return sum(v.astype(F32) for v in values)

    far0, far1, near1, near0, held_k, held_v = whole_call(
        query_back_kernel,
        (place, *dq_parts, w_query, key_weight, value_weight),
        [shape(BLOCK, 1024)] * 4 + [shape(2 * PAIR, HEAD)] * 2,
        [pltpu.VMEM((4, 1024, ROWS), BF16), pltpu.SemaphoreType.DMA((6,))],
        hbm=(5, 6, 7),
        flops=2 * 128 * 4096 * 512,
        traffic=8 << 20,
    )
    far_query = add(far1, to_core(far0)).astype(BF16)
    near_query = add(near0, to_core(near1)).astype(BF16)
    dkv_parts, far_query, near_query = lax.optimization_barrier(
        (dkv_parts, far_query, near_query)
    )

    far0, far1, dk, dv, dkv_own = whole_call(
        key_far_kernel,
        (place, dkv_parts, held_k, held_v, far_query),
        [shape(BLOCK, 1024), shape(BLOCK, 1024, kind=F32)]
        + [shape(BLOCK, HEAD)] * 2
        + [shape(BLOCK, 2 * HEAD)],
        flops=2 * 128 * 2048 * 256,
        traffic=2 << 20,
    )
    far_sum, dkv_own = lax.optimization_barrier(
        (add(far1, to_core(far0)).astype(BF16), dkv_own)
    )
    from_far = to_xl(far_sum)
    near1, near0 = whole_call(
        key_near_kernel,
        (place, dkv_own, held_k, held_v),
        [shape(BLOCK, 1024), shape(BLOCK, 1024, kind=F32)],
        flops=2 * 128 * 2048 * 256,
        traffic=2 << 20,
    )
    before = lax.optimization_barrier(add(from_far, near_query))
    input_grad = add(before, near0, to_core(near1)).astype(BF16)
    return input_grad, dk, dv


def solution(mesh):
    split = Mesh(mesh.devices.reshape(8, 4, 2, 2, 2), ("z", "y", "xh", "xl", "core"))
    ctx, tp = ("z", "y", "xh"), ("xl", "core")
    in_specs = (
        P(ctx, tp),
        P(ctx, tp),
        P(None, tp),
        P(None, tp),
        P(None, tp),
        P(tp, None),
        P(),
    )
    out_specs = (P(ctx, tp), P(ctx, tp), P(ctx, tp))
    return jax.shard_map(
        local, mesh=split, in_specs=in_specs, out_specs=out_specs, check_vma=False
    )
```

```python
import functools

import jax
import jax.numpy as jnp
from jax import lax
from jax.experimental import pallas as pl
from jax.experimental.pallas import tpu as pltpu
from jax.sharding import Mesh
from jax.sharding import PartitionSpec as P

HEAD = 128
FACTOR = HEAD**-0.5
LOG2E = 1.4426950408889634
SCALE2 = FACTOR * LOG2E
NEG_FILL = -1e30
LOWEST_TOP = -1e29
BLOCK = 128
HEADS = 4
ROWS = HEADS * BLOCK
CHUNK = 2 * BLOCK
FAR_FLOPS = 10_000_000_000
STEP = 512
STAT_FLOPS = 4 * 2048 * 2048 * 128
GRAD_FLOPS = 10 * 2048 * 2048 * 128
VMEM_LIMIT = 20 * 1024 * 1024
BF16 = jnp.bfloat16
F32 = jnp.float32


def shifted(size, step):
    return [(i, (i + step) % size) for i in range(size)]


def contract_last(left, right):
    return lax.dot_general(
        left, right, (((1,), (1,)), ((), ())), preferred_element_type=F32
    )


def matmul(left, right):
    return jnp.dot(left, right, preferred_element_type=F32)


PAIR = 2048


def near_kernel(
    place, x0, x1, g0, g1, wq, wk, wv, wo,
    x_half, g_half, far_q, far_k, far_v, far_o,
    near_q, near_k, near_v, near_o, g_buf, sems,
):
    xl, core = place[3], place[4]
    near = pl.ds(pl.multiple_of(xl * PAIR, PAIR), PAIR)
    far = pl.ds(pl.multiple_of((1 - xl) * PAIR, PAIR), PAIR)
    copies = []
    for rows, targets in (
        (near, (near_q, near_k, near_v, near_o)),
        (far, (far_q, far_k, far_v, far_o)),
    ):
        for source, target in zip((wq, wk, wv, wo), targets):
            part = source.at[:, rows] if source is wo else source.at[rows, :]
            copies.append(pltpu.make_async_copy(part, target, sems.at[len(copies)]))
    for copy in copies:
        copy.start()
    own, other = core_halves(core)
    for copy, weight, low, high in (
        (copies[0], near_q, 256, 768),
        (copies[1], near_k, 0, 128),
        (copies[2], near_v, 128, 256),
    ):
        copy.wait()
        x_half[:, low:high] = matmul(x0[...], weight[own, :]) + matmul(x1[...], weight[other, :])
    copies[3].wait()
    g_buf[...] = contract_last(g0[...], near_o[:, own]) + contract_last(g1[...], near_o[:, other])
    copies.append(pltpu.make_async_copy(g_buf, g_half, sems.at[8]))
    copies[8].start()
    for copy in copies[4:]:
        copy.wait()


def core_halves(core):
    return [pl.ds(pl.multiple_of(c * 1024, 1024), 1024) for c in (core, 1 - core)]


def far_inputs_kernel(place, x2, x3, wq, wk, wv, x_half, kv, q, kv_buf, q_buf, sems):
    own, other = core_halves(place[4])

    def product(weight, low, high):
        return (
            x_half[:, low:high]
            + matmul(x2[...], weight[own, :])
            + matmul(x3[...], weight[other, :])
        ).astype(BF16)

    kv_buf[:, :HEAD] = product(wk, 0, 128)
    kv_buf[:, HEAD:] = product(wv, 128, 256)
    copies = [pltpu.make_async_copy(kv_buf, kv.at[i], sems.at[i]) for i in range(16)]
    for copy in copies:
        copy.start()
    q_buf[...] = product(wq, 256, 768)
    copies.append(pltpu.make_async_copy(q_buf, q, sems.at[16]))
    copies[16].start()
    for copy in copies:
        copy.wait()


def far_grads_kernel(place, g2, g3, wo, g_half, q, out, g_buf, out_buf, sems):
    own, other = core_halves(place[4])
    fetch_g = pltpu.make_async_copy(g_half, g_buf, sems.at[0])
    fetch_q = pltpu.make_async_copy(q, out_buf.at[:, :ROWS], sems.at[1])
    fetch_g.start()
    fetch_q.start()
    far = contract_last(g2[...], wo[:, own]) + contract_last(g3[...], wo[:, other])
    fetch_g.wait()
    out_buf[:, ROWS:] = (g_buf[...] + far).astype(BF16)
    fetch_q.wait()
    store = pltpu.make_async_copy(out_buf, out, sems.at[2])
    store.start()
    store.wait()


def whole_call(
    kernel, operands, outs, scratch=(), hbm=(), hbm_outs=(), flops=0, traffic=0, exps=0
):
    vmem = pl.BlockSpec(memory_space=pltpu.VMEM)
    operands = list(operands)
    in_specs = [vmem] * len(operands)
    in_specs[0] = pl.BlockSpec(memory_space=pltpu.SMEM)
    for i in hbm:
        in_specs[i] = pl.BlockSpec(memory_space=pltpu.HBM)
        operands[i] = pltpu.with_memory_space_constraint(operands[i], pltpu.HBM)
    return pl.pallas_call(
        kernel,
        in_specs=in_specs,
        out_specs=[
            pl.BlockSpec(memory_space=pltpu.HBM) if i in hbm_outs else vmem
            for i in range(len(outs))
        ],
        out_shape=[
            pltpu.HBM(out.shape, out.dtype) if i in hbm_outs else out
            for i, out in enumerate(outs)
        ],
        scratch_shapes=list(scratch),
        compiler_params=pltpu.CompilerParams(vmem_limit_bytes=VMEM_LIMIT),
        cost_estimate=pl.CostEstimate(flops=flops, bytes_accessed=traffic, transcendentals=exps),
    )(*operands)


def stack_heads(ref, first):
    return jnp.concatenate(
        [ref[:, first + h * HEAD : first + (h + 1) * HEAD] for h in range(HEADS)], axis=0
    )


def visible(times, key_block, query_block):
    keys = jnp.broadcast_to(times[pl.ds(key_block, 1), :], (BLOCK, BLOCK)).T
    return jnp.where(keys <= times[pl.ds(query_block, 1), :], 0.0, NEG_FILL)


def stack_kernel(
    place, times_hbm, qd0, qd1, qd2, qd3, wk, wv,
    q_rows, g_rows, bias, far_kv, times, own, weights, sems,
):
    packs = []
    rows = pl.ds(pl.multiple_of((1 - place[3]) * PAIR, PAIR), PAIR)
    for k, weight in enumerate((wk, wv)):
        held = weights.at[k]
        fetched = pltpu.make_async_copy(weight.at[rows, :], held, sems.at[2 + 2 * k])
        packs.append((fetched, pltpu.make_async_copy(held, far_kv.at[k], sems.at[3 + 2 * k])))
    for fetched, _ in packs:
        fetched.start()
    copies = [
        pltpu.make_async_copy(qd0, own, sems.at[0]),
        pltpu.make_async_copy(times_hbm, times, sems.at[1]),
    ]
    for copy in copies:
        copy.start()
    for s, qd in ((1, qd1), (2, qd2), (3, qd3), (0, own)):
        if s == 0:
            copies[0].wait()
        q_rows[s * ROWS : (s + 1) * ROWS, :] = stack_heads(qd, 0)
        g_rows[s * ROWS : (s + 1) * ROWS, :] = stack_heads(qd, 512)
    for fetched, stored in packs:
        fetched.wait()
        stored.start()
    copies[1].wait()
    z, y, xh = place[0], place[1], place[2]
    for s in range(4):
        cols = slice(s * BLOCK, (s + 1) * BLOCK)
        query_block = 8 * z + 2 * ((y - s + 4) % 4) + xh
        for h in range(2):
            key_block = 8 * z + 2 * y + h
            bias[h * BLOCK : (h + 1) * BLOCK, cols] = visible(times, key_block, query_block)
    bias[2 * BLOCK :, :BLOCK] = visible(times, 8 * jnp.minimum(z + 1, 7), 8 * z + 7)
    bias[2 * BLOCK :, BLOCK:] = jnp.full((BLOCK, 3 * BLOCK), NEG_FILL, F32)
    for _, stored in packs:
        stored.wait()


def for_tiles(place, bias, tile, done):
    z, y, xh = place[0], place[1], place[2]

    def masked(part, s):
        return jnp.concatenate([bias[part, s * BLOCK : (s + 1) * BLOCK]] * HEADS, axis=1)

    for s in range(4):
        first = pl.multiple_of(z * CHUNK, CHUNK)
        tile(first, CHUNK, s * ROWS, ROWS, masked(slice(0, CHUNK), s))

    def past(first, keys):
        tile(pl.multiple_of(first, CHUNK), keys, 0, 4 * ROWS, None)

    def some(i, carry):
        past(i * STEP, STEP)
        done(i)
        return carry

    lax.fori_loop(0, z // 2, some, 0)

    @pl.when(z % 2 == 1)
    def _():
        past((z - 1) * CHUNK, CHUNK)

    @pl.when((z < 7) & (y == 0) & (xh == 1))
    def _():
        first = pl.multiple_of((z + 1) * CHUNK, CHUNK)
        tile(first, BLOCK, ROWS, ROWS, masked(slice(CHUNK, CHUNK + BLOCK), 0))


def stats_kernel(place, kv, q_rows, g_rows, bias, out):
    def tile(first, count, row, rows, hidden):
        cols = slice(row, row + rows)
        keys = kv[pl.ds(first, count), :HEAD]
        values = kv[pl.ds(first, count), HEAD:]
        scores = contract_last(keys, q_rows[cols, :]) * SCALE2
        first_visit = hidden is not None and count == CHUNK
        if hidden is not None:
            scores = scores + hidden
        top = jnp.maximum(jnp.max(scores, axis=0, keepdims=True), LOWEST_TOP)
        if not first_visit:
            old = out[0:1, cols]
            top = jnp.maximum(old, top)
        prob = jnp.exp2(scores - top)
        prob_grad = contract_last(values, g_rows[cols, :])
        norm = jnp.sum(prob, axis=0, keepdims=True)
        dot = jnp.sum(prob * prob_grad, axis=0, keepdims=True)
        if not first_visit:
            shrink = jnp.exp2(old - top)
            norm += out[1:2, cols] * shrink
            dot += out[2:3, cols] * shrink
        out[0:1, cols] = top
        out[1:2, cols] = norm
        out[2:3, cols] = dot

    out[3:4, :] = jnp.zeros((1, 4 * ROWS), F32)
    for_tiles(place, bias, tile, lambda i: None)


def stats(place, kv, rows):
    (out,) = whole_call(
        stats_kernel,
        (place, kv, *rows),
        [jax.ShapeDtypeStruct((4, 4 * ROWS), F32)],
        flops=STAT_FLOPS,
        traffic=2 << 20,
    )
    return out


def grads_kernel(
    place, kv, q_rows, g_rows, bias, st0, st1, st2, st3,
    dkv, dq0, dq1, dq2, dq3,
    sums, q_sum, row_stats, dkv_buf, dq_buf, out_sems,
):
    z = place[0]

    def clear(i, carry):
        dkv_buf[i] = jnp.zeros((BLOCK, 2 * HEAD), BF16)
        return carry

    lax.fori_loop(2 * z + 2, 16, clear, 0)
    for s in range(4):
        cols = slice(s * ROWS, (s + 1) * ROWS)
        tops, norms, dots = [], [], []
        for k, st in enumerate((st0, st1, st2, st3)):
            first = ((s - k) % 4) * ROWS
            tops.append(st[0:1, first : first + ROWS])
            norms.append(st[1:2, first : first + ROWS])
            dots.append(st[2:3, first : first + ROWS])
        top = functools.reduce(jnp.maximum, tops)
        scales = [jnp.exp2(t - top) for t in tops]
        norm = sum(n * f for n, f in zip(norms, scales))
        row_stats[0:1, cols] = top + jnp.log2(norm)
        row_stats[1:2, cols] = sum(d * f for d, f in zip(dots, scales)) / norm

    def tile(first, count, row, rows, hidden):
        cols = slice(row, row + rows)
        keys = kv[pl.ds(first, count), :HEAD]
        values = kv[pl.ds(first, count), HEAD:]
        q, g = q_rows[cols, :], g_rows[cols, :]
        scores = contract_last(keys, q) * SCALE2
        if hidden is not None:
            scores = scores + hidden
        prob = jnp.exp2(scores - row_stats[0:1, cols])
        prob_grad = contract_last(values, g)
        score_grad = (prob * (prob_grad - row_stats[1:2, cols])).astype(BF16)
        dk = matmul(score_grad, q)
        dv = matmul(prob.astype(BF16), g)
        dq = lax.dot_general(
            keys, score_grad, (((0,), (0,)), ((), ())), preferred_element_type=F32
        )
        block = first // BLOCK
        if hidden is not None and count == CHUNK:
            q_sum[:, cols] = dq
            if row:
                dk += sums[:, :HEAD]
                dv += sums[:, HEAD:]
            sums[:, :HEAD] = dk
            sums[:, HEAD:] = dv
            if row < 3 * ROWS:
                return
        else:
            q_sum[:, cols] += dq
        for i in range(count // BLOCK):
            part = slice(i * BLOCK, (i + 1) * BLOCK)
            dkv_buf[block + i, :, :HEAD] = dk[part, :].astype(BF16)
            dkv_buf[block + i, :, HEAD:] = dv[part, :].astype(BF16)

    def send(i):
        part = pl.ds(4 * i, 4)
        return pltpu.make_async_copy(dkv_buf.at[part], dkv.at[part], out_sems.at[i])

    for_tiles(place, bias, tile, lambda i: send(i).start())
    for i in range(4):

        @pl.when(i >= z // 2)
        def _():
            send(i).start()

    outs = []
    for s, dq in enumerate((dq0, dq1, dq2, dq3)):
        for h in range(HEADS):
            part = q_sum[:, s * ROWS + h * HEAD : s * ROWS + (h + 1) * HEAD]
            dq_buf[s, :, h * HEAD : (h + 1) * HEAD] = (part.T * FACTOR).astype(BF16)
        outs.append(pltpu.make_async_copy(dq_buf.at[s], dq, out_sems.at[4 + s]))
        outs[-1].start()
    for i in range(4):
        send(i).wait()
    for copy in outs:
        copy.wait()


def grads(place, kv, rows, gathered):
    return whole_call(
        grads_kernel,
        (place, kv, *rows, *gathered),
        [jax.ShapeDtypeStruct((16, BLOCK, 2 * HEAD), BF16)]
        + [jax.ShapeDtypeStruct((BLOCK, ROWS), BF16)] * 4,
        [
            pltpu.VMEM((CHUNK, 2 * HEAD), F32),
            pltpu.VMEM((HEAD, 4 * ROWS), F32),
            pltpu.VMEM((8, 4 * ROWS), F32),
            pltpu.VMEM((16, BLOCK, 2 * HEAD), BF16),
            pltpu.VMEM((4, BLOCK, ROWS), BF16),
            pltpu.SemaphoreType.DMA((8,)),
        ],
        hbm_outs=(0, 1, 2, 3, 4),
        flops=GRAD_FLOPS,
        traffic=4 << 20,
    )


def feature_rows(place, flip):
    first = (2 * place[3] + place[4]) ^ flip
    return pl.ds(pl.multiple_of(first * 1024, 1024), 1024)


def query_back_kernel(
    place, dq0, dq1, dq2, dq3, wq, wk, wv, got_kv, far0, far1, near1, near0, out_kv, held, sems
):
    copies = [
        pltpu.make_async_copy(wq.at[feature_rows(place, flip), :], held.at[i], sems.at[i])
        for i, flip in enumerate((3, 2, 1, 0))
    ]
    rows = pl.ds(pl.multiple_of(place[3] * PAIR, PAIR), PAIR)
    sources = (wk.at[rows, :], wv.at[rows, :], got_kv.at[0], got_kv.at[1])
    for i, source in enumerate(sources):
        low = (i % 2) * HEAD
        target = out_kv.at[i // 2, :, low : low + HEAD]
        copies.append(pltpu.make_async_copy(source, target, sems.at[4 + i]))
    for copy in copies:
        copy.start()
    parts = [d[...].astype(F32) for d in (dq0, dq1, dq2, dq3)]
    total = (parts[0] + parts[1] + parts[2] + parts[3]).astype(BF16)
    for i, out in enumerate((far0, far1, near1, near0)):
        copies[i].wait()
        out[...] = contract_last(total, held[i]).astype(out.dtype)
    for copy in copies[4:]:
        copy.wait()


def key_sum_kernel(place, parts, dk, dv, dkv):
    total = parts[0].astype(F32)
    for i in range(1, 16):
        total = total + parts[i].astype(F32)
    dk[...] = (total[:, :HEAD] * FACTOR).astype(BF16)
    dv[...] = total[:, HEAD:].astype(BF16)
    dkv[:, :HEAD] = dk[...]
    dkv[:, HEAD:] = dv[...]


def key_near_kernel(place, dkv, weights, queries, own, other):
    mine, siblings = core_halves(place[4])
    own[...] = queries[...].astype(F32) + contract_last(dkv[...], weights[0, mine, :])
    other[...] = contract_last(dkv[...], weights[0, siblings, :])


def key_far_kernel(place, dkv, weights, own, other, queries, own_out, other_out):
    mine, siblings = core_halves(place[4])
    other_out[...] = (other[...] + contract_last(dkv[...], weights[1, siblings, :])).astype(BF16)
    own_out[...] = (
        own[...] + queries[...].astype(F32) + contract_last(dkv[...], weights[1, mine, :])
    )


def local(inputs, out_grad, w_query, key_weight, value_weight, w_output, times):
    axes = ("z", "y", "xh", "xl", "core")
    place = jnp.stack([lax.axis_index(name) for name in axes]).astype(jnp.int32)
    times2d = times.reshape(64, BLOCK)
    swap = shifted(2, 1)

    def to_core(value):
        return lax.ppermute(value, "core", swap)

    def to_xl(value):
        return lax.ppermute(value, "xl", swap)

    def shape(*dims, kind=BF16):
        return jax.ShapeDtypeStruct(dims, kind)

    x2, g2 = to_xl(inputs), to_xl(out_grad)
    x1, g1 = to_core(inputs), to_core(out_grad)
    held = [
        shape(PAIR, ROWS), shape(PAIR, HEAD), shape(PAIR, HEAD), shape(ROWS, PAIR)
    ]
    x_half, g_half, far_q, far_k, far_v, far_o = whole_call(
        near_kernel,
        (place, inputs, x1, out_grad, g1, w_query, key_weight, value_weight, w_output),
        [shape(BLOCK, 768, kind=F32), shape(BLOCK, ROWS, kind=F32)] + held,
        [pltpu.VMEM(h.shape, BF16) for h in held]
        + [pltpu.VMEM((BLOCK, ROWS), F32), pltpu.SemaphoreType.DMA((9,))],
        hbm=(5, 6, 7, 8),
        hbm_outs=(1,),
        flops=2 * 128 * 2048 * 1280,
        traffic=10 << 20,
    )
    x2, x_half, g_half = lax.optimization_barrier((x2, x_half, g_half))
    x3 = to_core(x2)
    kv_own, q_own = whole_call(
        far_inputs_kernel,
        (place, x2, x3, far_q, far_k, far_v, x_half),
        [shape(16, BLOCK, 2 * HEAD), shape(BLOCK, ROWS)],
        [
            pltpu.VMEM((BLOCK, 2 * HEAD), BF16),
            pltpu.VMEM((BLOCK, ROWS), BF16),
            pltpu.SemaphoreType.DMA((17,)),
        ],
        hbm_outs=(0, 1),
        flops=2 * 128 * 2048 * 768,
        traffic=4 << 20,
    )
    g2, q_own = lax.optimization_barrier((g2, q_own))
    g3 = to_core(g2)
    (qd_own,) = whole_call(
        far_grads_kernel,
        (place, g2, g3, far_o, g_half, q_own),
        [shape(BLOCK, 1024)],
        [
            pltpu.VMEM((BLOCK, ROWS), F32),
            pltpu.VMEM((BLOCK, 1024), BF16),
            pltpu.SemaphoreType.DMA((3,)),
        ],
        hbm=(4, 5),
        hbm_outs=(0,),
        flops=FAR_FLOPS,
        traffic=3 << 20,
    )
    kv = lax.all_to_all(kv_own, ("z", "xh"), 0, 0, tiled=True).reshape(16 * BLOCK, 2 * HEAD)
    blocks = [qd_own] + [lax.ppermute(qd_own, "y", shifted(4, s)) for s in (1, 2, 3)]

    *rows, far_kv = whole_call(
        stack_kernel,
        (place, times2d, *blocks, key_weight, value_weight),
        [shape(4 * ROWS, HEAD)] * 2
        + [shape(CHUNK + BLOCK, ROWS, kind=F32)]
        + [shape(2, PAIR, HEAD)],
        [
            pltpu.VMEM((64, BLOCK), jnp.int32),
            pltpu.VMEM((BLOCK, 1024), BF16),
            pltpu.VMEM((2, PAIR, HEAD), BF16),
            pltpu.SemaphoreType.DMA((6,)),
        ],
        hbm=(1, 2, 6, 7),
        hbm_outs=(3,),
        traffic=2 << 20,
    )
    got_kv = to_xl(far_kv)
    own_stats = stats(place, kv, rows)
    gathered = [own_stats] + [lax.ppermute(own_stats, "y", shifted(4, s)) for s in (1, 2, 3)]
    dkv, *dqs = grads(place, kv, rows, gathered)

    dkv, got_kv = lax.optimization_barrier((dkv, got_kv))
    dkv_parts = lax.all_to_all(dkv, ("z", "xh"), 0, 0, tiled=True)
    dq_parts = [dqs[0]] + [lax.ppermute(dqs[s], "y", shifted(4, -s)) for s in (1, 2, 3)]

    def add(*values):
        return sum(v.astype(F32) for v in values)

    far0, far1, near1, near0, held_kv = whole_call(
        query_back_kernel,
        (place, *dq_parts, w_query, key_weight, value_weight, got_kv),
        [shape(BLOCK, 1024)] * 4 + [shape(2, PAIR, 2 * HEAD)],
        [pltpu.VMEM((4, 1024, ROWS), BF16), pltpu.SemaphoreType.DMA((8,))],
        hbm=(5, 6, 7, 8),
        flops=2 * 128 * 4096 * 512,
        traffic=8 << 20,
    )
    far_queries = to_xl(add(far1, to_core(far0)).astype(BF16))
    near_queries = add(near0, to_core(near1)).astype(BF16)
    dkv_parts, near_queries = lax.optimization_barrier((dkv_parts, near_queries))

    dk, dv, dkv_own = whole_call(
        key_sum_kernel,
        (place, dkv_parts),
        [shape(BLOCK, HEAD)] * 2 + [shape(BLOCK, 2 * HEAD)],
        traffic=2 << 20,
    )
    dkv_far = to_xl(dkv_own)
    halves = [shape(BLOCK, 1024, kind=F32)] * 2
    own_half, other_half = whole_call(
        key_near_kernel,
        (place, dkv_own, held_kv, near_queries),
        halves,
        flops=2 * 128 * 256 * 2048,
        traffic=2 << 20,
    )
    own_half, other_half = whole_call(
        key_far_kernel,
        (place, dkv_far, held_kv, own_half, other_half, far_queries),
        [halves[0], shape(BLOCK, 1024)],
        flops=2 * 128 * 256 * 2048,
        traffic=2 << 20,
    )
    input_grad = add(own_half, to_core(other_half)).astype(BF16)
    return input_grad, dk, dv


def solution(mesh):
    split = Mesh(mesh.devices.reshape(8, 4, 2, 2, 2), ("z", "y", "xh", "xl", "core"))
    ctx, tp = ("z", "y", "xh"), ("xl", "core")
    in_specs = (
        P(ctx, tp),
        P(ctx, tp),
        P(None, tp),
        P(None, tp),
        P(None, tp),
        P(tp, None),
        P(),
    )
    out_specs = (P(ctx, tp), P(ctx, tp), P(ctx, tp))
    return jax.shard_map(
        local, mesh=split, in_specs=in_specs, out_specs=out_specs, check_vma=False
    )
```

```python
import functools

import jax
import jax.numpy as jnp
from jax import lax
from jax.experimental import pallas as pl
from jax.experimental.pallas import tpu as pltpu
from jax.sharding import Mesh
from jax.sharding import PartitionSpec as P

HEAD = 128
FACTOR = HEAD**-0.5
LOG2E = 1.4426950408889634
SCALE2 = FACTOR * LOG2E
NEG_FILL = -1e30
LOWEST_TOP = -1e29
BLOCK = 128
HEADS = 4
ROWS = HEADS * BLOCK
CHUNK = 2 * BLOCK
FAR_FLOPS = 10_000_000_000
STEP = 512
NEAR_FLOPS = 2 * 128 * 2048 * 512
STAT_FLOPS = 4 * 2048 * 2048 * 128
GRAD_FLOPS = 10 * 2048 * 2048 * 128
VMEM_LIMIT = 20 * 1024 * 1024
BF16 = jnp.bfloat16
F32 = jnp.float32


def shifted(size, step):
    return [(i, (i + step) % size) for i in range(size)]


def contract_last(left, right):
    return lax.dot_general(
        left, right, (((1,), (1,)), ((), ())), preferred_element_type=F32
    )


def matmul(left, right):
    return jnp.dot(left, right, preferred_element_type=F32)


PAIR = 2048


def near_kernel(
    place, x0, x1, g0, g1, wq, wk, wv, wo,
    x_half, g_half, far_q, far_k, far_v, far_o,
    near_q, near_k, near_v, near_o, g_buf, sems,
):
    xl, core = place[3], place[4]
    near = pl.ds(pl.multiple_of(xl * PAIR, PAIR), PAIR)
    far = pl.ds(pl.multiple_of((1 - xl) * PAIR, PAIR), PAIR)
    copies = []
    for rows, targets in (
        (near, (near_q, near_k, near_v, near_o)),
        (far, (far_q, far_k, far_v, far_o)),
    ):
        for source, target in zip((wq, wk, wv, wo), targets):
            part = source.at[:, rows] if source is wo else source.at[rows, :]
            copies.append(pltpu.make_async_copy(part, target, sems.at[len(copies)]))
    for copy in copies:
        copy.start()
    own, other = core_halves(core)
    for copy, weight, low, high in (
        (copies[0], near_q, 256, 768),
        (copies[1], near_k, 0, 128),
        (copies[2], near_v, 128, 256),
    ):
        copy.wait()
        x_half[:, low:high] = matmul(x0[...], weight[own, :]) + matmul(x1[...], weight[other, :])
    copies[3].wait()
    g_buf[...] = contract_last(g0[...], near_o[:, own]) + contract_last(g1[...], near_o[:, other])
    copies.append(pltpu.make_async_copy(g_buf, g_half, sems.at[8]))
    copies[8].start()
    for copy in copies[4:]:
        copy.wait()


def core_halves(core):
    return [pl.ds(pl.multiple_of(c * 1024, 1024), 1024) for c in (core, 1 - core)]


def far_inputs_kernel(place, x2, x3, wq, wk, wv, x_half, kv, q, kv_buf, q_buf, sems):
    own, other = core_halves(place[4])

    def product(weight, low, high):
        return (
            x_half[:, low:high]
            + matmul(x2[...], weight[own, :])
            + matmul(x3[...], weight[other, :])
        ).astype(BF16)

    pair = jnp.concatenate([product(wk, 0, 128), product(wv, 128, 256)], axis=1)
    for i in range(4):
        kv_buf[i] = pair
    copies = [
        pltpu.make_async_copy(kv_buf, kv.at[pl.ds(4 * i, 4)], sems.at[i]) for i in range(4)
    ]
    for copy in copies:
        copy.start()
    q_buf[...] = product(wq, 256, 768)
    copies.append(pltpu.make_async_copy(q_buf, q, sems.at[4]))
    copies[4].start()
    for copy in copies:
        copy.wait()


def far_grads_kernel(place, g2, g3, wo, g_half, q, out, g_buf, out_buf, sems):
    own, other = core_halves(place[4])
    fetch_g = pltpu.make_async_copy(g_half, g_buf, sems.at[0])
    fetch_q = pltpu.make_async_copy(q, out_buf.at[:, :ROWS], sems.at[1])
    fetch_g.start()
    fetch_q.start()
    far = contract_last(g2[...], wo[:, own]) + contract_last(g3[...], wo[:, other])
    fetch_g.wait()
    out_buf[:, ROWS:] = (g_buf[...] + far).astype(BF16)
    fetch_q.wait()
    store = pltpu.make_async_copy(out_buf, out, sems.at[2])
    store.start()
    store.wait()


def whole_call(
    kernel, operands, outs, scratch=(), hbm=(), hbm_outs=(), flops=0, traffic=0, exps=0
):
    vmem = pl.BlockSpec(memory_space=pltpu.VMEM)
    operands = list(operands)
    in_specs = [vmem] * len(operands)
    in_specs[0] = pl.BlockSpec(memory_space=pltpu.SMEM)
    for i in hbm:
        in_specs[i] = pl.BlockSpec(memory_space=pltpu.HBM)
        operands[i] = pltpu.with_memory_space_constraint(operands[i], pltpu.HBM)
    return pl.pallas_call(
        kernel,
        in_specs=in_specs,
        out_specs=[
            pl.BlockSpec(memory_space=pltpu.HBM) if i in hbm_outs else vmem
            for i in range(len(outs))
        ],
        out_shape=[
            pltpu.HBM(out.shape, out.dtype) if i in hbm_outs else out
            for i, out in enumerate(outs)
        ],
        scratch_shapes=list(scratch),
        compiler_params=pltpu.CompilerParams(vmem_limit_bytes=VMEM_LIMIT),
        cost_estimate=pl.CostEstimate(flops=flops, bytes_accessed=traffic, transcendentals=exps),
    )(*operands)


def stack_heads(ref, first):
    return jnp.concatenate(
        [ref[:, first + h * HEAD : first + (h + 1) * HEAD] for h in range(HEADS)], axis=0
    )


def visible(times, key_block, query_block):
    keys = jnp.broadcast_to(times[pl.ds(key_block, 1), :], (BLOCK, BLOCK)).T
    return jnp.where(keys <= times[pl.ds(query_block, 1), :], 0.0, NEG_FILL)


def stack_kernel(
    place, times_hbm, qd0, qd1, qd2, qd3, wk, wv,
    q_rows, g_rows, bias, far_kv, times, own, weights, sems,
):
    packs = []
    rows = pl.ds(pl.multiple_of((1 - place[3]) * PAIR, PAIR), PAIR)
    for k, weight in enumerate((wk, wv)):
        held = weights.at[k]
        fetched = pltpu.make_async_copy(weight.at[rows, :], held, sems.at[2 + 2 * k])
        packs.append((fetched, pltpu.make_async_copy(held, far_kv.at[k], sems.at[3 + 2 * k])))
    for fetched, _ in packs:
        fetched.start()
    copies = [
        pltpu.make_async_copy(qd0, own, sems.at[0]),
        pltpu.make_async_copy(times_hbm, times, sems.at[1]),
    ]
    for copy in copies:
        copy.start()
    for s, qd in ((1, qd1), (2, qd2), (3, qd3), (0, own)):
        if s == 0:
            copies[0].wait()
        q_rows[s * ROWS : (s + 1) * ROWS, :] = stack_heads(qd, 0)
        g_rows[s * ROWS : (s + 1) * ROWS, :] = stack_heads(qd, 512)
    for fetched, stored in packs:
        fetched.wait()
        stored.start()
    copies[1].wait()
    z, y, xh = place[0], place[1], place[2]
    for s in range(4):
        cols = slice(s * BLOCK, (s + 1) * BLOCK)
        query_block = 8 * z + 2 * ((y - s + 4) % 4) + xh
        for h in range(2):
            key_block = 8 * z + 2 * y + h
            bias[h * BLOCK : (h + 1) * BLOCK, cols] = visible(times, key_block, query_block)
    bias[2 * BLOCK :, :BLOCK] = visible(times, 8 * jnp.minimum(z + 1, 7), 8 * z + 7)
    bias[2 * BLOCK :, BLOCK:] = jnp.full((BLOCK, 3 * BLOCK), NEG_FILL, F32)
    for _, stored in packs:
        stored.wait()


def for_tiles(place, bias, tile, done):
    z, y, xh = place[0], place[1], place[2]

    def masked(part, s):
        return jnp.concatenate([bias[part, s * BLOCK : (s + 1) * BLOCK]] * HEADS, axis=1)

    for s in range(4):
        first = pl.multiple_of(z * CHUNK, CHUNK)
        tile(first, CHUNK, s * ROWS, ROWS, masked(slice(0, CHUNK), s))

    def past(first, keys):
        tile(pl.multiple_of(first, CHUNK), keys, 0, 4 * ROWS, None)

    def some(i, carry):
        past(i * STEP, STEP)
        done(i)
        return carry

    lax.fori_loop(0, z // 2, some, 0)

    @pl.when(z % 2 == 1)
    def _():
        past((z - 1) * CHUNK, CHUNK)

    @pl.when((z < 7) & (y == 0) & (xh == 1))
    def _():
        first = pl.multiple_of((z + 1) * CHUNK, CHUNK)
        tile(first, BLOCK, ROWS, ROWS, masked(slice(CHUNK, CHUNK + BLOCK), 0))


def stats_kernel(place, kv, q_rows, g_rows, bias, out):
    def tile(first, count, row, rows, hidden):
        cols = slice(row, row + rows)
        keys = kv[pl.ds(first, count), :HEAD]
        values = kv[pl.ds(first, count), HEAD:]
        scores = contract_last(keys, q_rows[cols, :]) * SCALE2
        first_visit = hidden is not None and count == CHUNK
        if hidden is not None:
            scores = scores + hidden
        top = jnp.maximum(jnp.max(scores, axis=0, keepdims=True), LOWEST_TOP)
        if not first_visit:
            old = out[0:1, cols]
            top = jnp.maximum(old, top)
        prob = jnp.exp2(scores - top)
        prob_grad = contract_last(values, g_rows[cols, :])
        norm = jnp.sum(prob, axis=0, keepdims=True)
        dot = jnp.sum(prob * prob_grad, axis=0, keepdims=True)
        if not first_visit:
            shrink = jnp.exp2(old - top)
            norm += out[1:2, cols] * shrink
            dot += out[2:3, cols] * shrink
        out[0:1, cols] = top
        out[1:2, cols] = norm
        out[2:3, cols] = dot

    out[3:4, :] = jnp.zeros((1, 4 * ROWS), F32)
    for_tiles(place, bias, tile, lambda i: None)


def stats(place, kv, rows):
    (out,) = whole_call(
        stats_kernel,
        (place, kv, *rows),
        [jax.ShapeDtypeStruct((4, 4 * ROWS), F32)],
        flops=STAT_FLOPS,
        traffic=2 << 20,
    )
    return out


def grads_kernel(
    place, kv, q_rows, g_rows, bias, st0, st1, st2, st3,
    dkv, dq0, dq1, dq2, dq3,
    sums, q_sum, row_stats, dkv_buf, dq_buf, out_sems,
):
    z = place[0]

    def clear(i, carry):
        dkv_buf[i] = jnp.zeros((BLOCK, 2 * HEAD), BF16)
        return carry

    lax.fori_loop(2 * z + 2, 16, clear, 0)
    for s in range(4):
        cols = slice(s * ROWS, (s + 1) * ROWS)
        tops, norms, dots = [], [], []
        for k, st in enumerate((st0, st1, st2, st3)):
            first = ((s - k) % 4) * ROWS
            tops.append(st[0:1, first : first + ROWS])
            norms.append(st[1:2, first : first + ROWS])
            dots.append(st[2:3, first : first + ROWS])
        top = functools.reduce(jnp.maximum, tops)
        scales = [jnp.exp2(t - top) for t in tops]
        norm = sum(n * f for n, f in zip(norms, scales))
        row_stats[0:1, cols] = top + jnp.log2(norm)
        row_stats[1:2, cols] = sum(d * f for d, f in zip(dots, scales)) / norm

    def tile(first, count, row, rows, hidden):
        cols = slice(row, row + rows)
        keys = kv[pl.ds(first, count), :HEAD]
        values = kv[pl.ds(first, count), HEAD:]
        q, g = q_rows[cols, :], g_rows[cols, :]
        scores = contract_last(keys, q) * SCALE2
        if hidden is not None:
            scores = scores + hidden
        prob = jnp.exp2(scores - row_stats[0:1, cols])
        prob_grad = contract_last(values, g)
        score_grad = (prob * (prob_grad - row_stats[1:2, cols])).astype(BF16)
        dk = matmul(score_grad, q)
        dv = matmul(prob.astype(BF16), g)
        dq = lax.dot_general(
            keys, score_grad, (((0,), (0,)), ((), ())), preferred_element_type=F32
        )
        block = first // BLOCK
        if hidden is not None and count == CHUNK:
            q_sum[:, cols] = dq
            if row:
                dk += sums[:, :HEAD]
                dv += sums[:, HEAD:]
            sums[:, :HEAD] = dk
            sums[:, HEAD:] = dv
            if row < 3 * ROWS:
                return
        else:
            q_sum[:, cols] += dq
        for i in range(count // BLOCK):
            part = slice(i * BLOCK, (i + 1) * BLOCK)
            dkv_buf[block + i, :, :HEAD] = dk[part, :].astype(BF16)
            dkv_buf[block + i, :, HEAD:] = dv[part, :].astype(BF16)

    def send(i):
        part = pl.ds(4 * i, 4)
        return pltpu.make_async_copy(dkv_buf.at[part], dkv.at[part], out_sems.at[i])

    for_tiles(place, bias, tile, lambda i: send(i).start())
    for i in range(4):

        @pl.when(i >= z // 2)
        def _():
            send(i).start()

    outs = []
    for s, dq in enumerate((dq0, dq1, dq2, dq3)):
        for h in range(HEADS):
            part = q_sum[:, s * ROWS + h * HEAD : s * ROWS + (h + 1) * HEAD]
            dq_buf[s, :, h * HEAD : (h + 1) * HEAD] = (part.T * FACTOR).astype(BF16)
        outs.append(pltpu.make_async_copy(dq_buf.at[s], dq, out_sems.at[4 + s]))
        outs[-1].start()
    for i in range(4):
        send(i).wait()
    for copy in outs:
        copy.wait()


def grads(place, kv, rows, gathered):
    return whole_call(
        grads_kernel,
        (place, kv, *rows, *gathered),
        [jax.ShapeDtypeStruct((16, BLOCK, 2 * HEAD), BF16)]
        + [jax.ShapeDtypeStruct((BLOCK, ROWS), BF16)] * 4,
        [
            pltpu.VMEM((CHUNK, 2 * HEAD), F32),
            pltpu.VMEM((HEAD, 4 * ROWS), F32),
            pltpu.VMEM((8, 4 * ROWS), F32),
            pltpu.VMEM((16, BLOCK, 2 * HEAD), BF16),
            pltpu.VMEM((4, BLOCK, ROWS), BF16),
            pltpu.SemaphoreType.DMA((8,)),
        ],
        hbm_outs=(0, 1, 2, 3, 4),
        flops=GRAD_FLOPS,
        traffic=4 << 20,
    )


def feature_rows(place, flip):
    first = (2 * place[3] + place[4]) ^ flip
    return pl.ds(pl.multiple_of(first * 1024, 1024), 1024)


def query_far_kernel(place, dq0, dq1, dq2, dq3, wq, far0, far1, total, held, sems):
    copies = [
        pltpu.make_async_copy(wq.at[feature_rows(place, flip), :], held.at[i], sems.at[i])
        for i, flip in enumerate((3, 2))
    ]
    for copy in copies:
        copy.start()
    parts = [d[...].astype(F32) for d in (dq0, dq1, dq2, dq3)]
    total[...] = (parts[0] + parts[1] + parts[2] + parts[3]).astype(BF16)
    for copy, block, out in zip(copies, (0, 1), (far0, far1)):
        copy.wait()
        out[...] = contract_last(total[...], held[block]).astype(out.dtype)


def query_near_kernel(place, total, wq, wk, wv, got_kv, near1, near0, out_kv, held, sems):
    copies = [
        pltpu.make_async_copy(wq.at[feature_rows(place, flip), :], held.at[i], sems.at[i])
        for i, flip in enumerate((1, 0))
    ]
    rows = pl.ds(pl.multiple_of(place[3] * PAIR, PAIR), PAIR)
    sources = (wk.at[rows, :], wv.at[rows, :], got_kv.at[0], got_kv.at[1])
    for i, source in enumerate(sources):
        low = (i % 2) * HEAD
        target = out_kv.at[i // 2, :, low : low + HEAD]
        copies.append(pltpu.make_async_copy(source, target, sems.at[2 + i]))
    for copy in copies:
        copy.start()
    for copy, block, out in zip(copies, (0, 1), (near1, near0)):
        copy.wait()
        out[...] = contract_last(total[...], held[block]).astype(out.dtype)
    for copy in copies[2:]:
        copy.wait()


def key_sum_kernel(place, parts, dk, dv, dkv):
    total = parts[0].astype(F32)
    for i in range(1, 16):
        total = total + parts[i].astype(F32)
    dk[...] = (total[:, :HEAD] * FACTOR).astype(BF16)
    dv[...] = total[:, HEAD:].astype(BF16)
    dkv[:, :HEAD] = dk[...]
    dkv[:, HEAD:] = dv[...]


def key_near_kernel(place, dkv, weights, queries, far_queries, own, other):
    mine, siblings = core_halves(place[4])
    total = queries[...].astype(F32) + far_queries[...].astype(F32)
    own[...] = total + contract_last(dkv[...], weights[0, mine, :])
    other[...] = contract_last(dkv[...], weights[0, siblings, :])


def key_far_kernel(flip, place, dkv, weights, before, out):
    rows = core_halves(place[4])[flip]
    out[...] = (before[...] + contract_last(dkv[...], weights[1, rows, :])).astype(out.dtype)


def local(inputs, out_grad, w_query, key_weight, value_weight, w_output, times):
    axes = ("z", "y", "xh", "xl", "core")
    place = jnp.stack([lax.axis_index(name) for name in axes]).astype(jnp.int32)
    times2d = times.reshape(64, BLOCK)
    swap = shifted(2, 1)

    def to_core(value):
        return lax.ppermute(value, "core", swap)

    def to_xl(value):
        return lax.ppermute(value, "xl", swap)

    def shape(*dims, kind=BF16):
        return jax.ShapeDtypeStruct(dims, kind)

    x2, g2 = to_xl(inputs), to_xl(out_grad)
    x1, g1 = to_core(inputs), to_core(out_grad)
    held = [
        shape(PAIR, ROWS), shape(PAIR, HEAD), shape(PAIR, HEAD), shape(ROWS, PAIR)
    ]
    x_half, g_half, far_q, far_k, far_v, far_o = whole_call(
        near_kernel,
        (place, inputs, x1, out_grad, g1, w_query, key_weight, value_weight, w_output),
        [shape(BLOCK, 768, kind=F32), shape(BLOCK, ROWS, kind=F32)] + held,
        [pltpu.VMEM(h.shape, BF16) for h in held]
        + [pltpu.VMEM((BLOCK, ROWS), F32), pltpu.SemaphoreType.DMA((9,))],
        hbm=(5, 6, 7, 8),
        hbm_outs=(1,),
        flops=2 * 128 * 2048 * 1280,
        traffic=10 << 20,
    )
    x2, x_half, g_half = lax.optimization_barrier((x2, x_half, g_half))
    x3 = to_core(x2)
    kv_own, q_own = whole_call(
        far_inputs_kernel,
        (place, x2, x3, far_q, far_k, far_v, x_half),
        [shape(16, BLOCK, 2 * HEAD), shape(BLOCK, ROWS)],
        [
            pltpu.VMEM((4, BLOCK, 2 * HEAD), BF16),
            pltpu.VMEM((BLOCK, ROWS), BF16),
            pltpu.SemaphoreType.DMA((5,)),
        ],
        hbm_outs=(0, 1),
        flops=2 * 128 * 2048 * 768,
        traffic=4 << 20,
    )
    g2, q_own = lax.optimization_barrier((g2, q_own))
    g3 = to_core(g2)
    (qd_own,) = whole_call(
        far_grads_kernel,
        (place, g2, g3, far_o, g_half, q_own),
        [shape(BLOCK, 1024)],
        [
            pltpu.VMEM((BLOCK, ROWS), F32),
            pltpu.VMEM((BLOCK, 1024), BF16),
            pltpu.SemaphoreType.DMA((3,)),
        ],
        hbm=(4, 5),
        hbm_outs=(0,),
        flops=FAR_FLOPS,
        traffic=3 << 20,
    )
    kv = lax.all_to_all(kv_own, ("z", "xh"), 0, 0, tiled=True).reshape(16 * BLOCK, 2 * HEAD)
    blocks = [qd_own] + [lax.ppermute(qd_own, "y", shifted(4, s)) for s in (1, 2, 3)]

    *rows, far_kv = whole_call(
        stack_kernel,
        (place, times2d, *blocks, key_weight, value_weight),
        [shape(4 * ROWS, HEAD)] * 2
        + [shape(CHUNK + BLOCK, ROWS, kind=F32)]
        + [shape(2, PAIR, HEAD)],
        [
            pltpu.VMEM((64, BLOCK), jnp.int32),
            pltpu.VMEM((BLOCK, 1024), BF16),
            pltpu.VMEM((2, PAIR, HEAD), BF16),
            pltpu.SemaphoreType.DMA((6,)),
        ],
        hbm=(1, 2, 6, 7),
        hbm_outs=(3,),
        traffic=2 << 20,
    )
    got_kv = to_xl(far_kv)
    own_stats = stats(place, kv, rows)
    gathered = [own_stats] + [lax.ppermute(own_stats, "y", shifted(4, s)) for s in (1, 2, 3)]
    dkv, *dqs = grads(place, kv, rows, gathered)

    dkv, got_kv = lax.optimization_barrier((dkv, got_kv))
    dkv_parts = lax.all_to_all(dkv, ("z", "xh"), 0, 0, tiled=True)
    dq_parts = [dqs[0]] + [lax.ppermute(dqs[s], "y", shifted(4, -s)) for s in (1, 2, 3)]

    def add(*values):
        return sum(v.astype(F32) for v in values)

    far0, far1, dq = whole_call(
        query_far_kernel,
        (place, *dq_parts, w_query),
        [shape(BLOCK, 1024)] * 2 + [shape(BLOCK, ROWS)],
        [pltpu.VMEM((2, 1024, ROWS), BF16), pltpu.SemaphoreType.DMA((2,))],
        hbm=(5,),
        flops=2 * 128 * 2048 * 512,
        traffic=2 << 20,
    )
    far_sum = add(far1, to_core(far0)).astype(BF16)
    far_sum, dq = lax.optimization_barrier((far_sum, dq))
    far_queries = to_xl(far_sum)
    near1, near0, held_kv = whole_call(
        query_near_kernel,
        (place, dq, w_query, key_weight, value_weight, got_kv),
        [shape(BLOCK, 1024)] * 2 + [shape(2, PAIR, 2 * HEAD)],
        [pltpu.VMEM((2, 1024, ROWS), BF16), pltpu.SemaphoreType.DMA((6,))],
        hbm=(2, 3, 4, 5),
        flops=NEAR_FLOPS,
        traffic=4 << 20,
    )
    near_queries = add(near0, to_core(near1)).astype(BF16)
    dkv_parts, near_queries = lax.optimization_barrier((dkv_parts, near_queries))

    dk, dv, dkv_own = whole_call(
        key_sum_kernel,
        (place, dkv_parts),
        [shape(BLOCK, HEAD)] * 2 + [shape(BLOCK, 2 * HEAD)],
        traffic=2 << 20,
    )
    dkv_far = to_xl(dkv_own)
    halves = [shape(BLOCK, 1024, kind=F32)] * 2
    own_half, other_half = whole_call(
        key_near_kernel,
        (place, dkv_own, held_kv, near_queries, far_queries),
        halves,
        flops=2 * 128 * 256 * 2048,
        traffic=2 << 20,
    )
    (other_half,) = whole_call(
        functools.partial(key_far_kernel, 1),
        (place, dkv_far, held_kv, other_half),
        [shape(BLOCK, 1024)],
        flops=2 * 128 * 256 * 1024,
        traffic=1 << 20,
    )
    got_half = to_core(other_half)
    (own_half,) = whole_call(
        functools.partial(key_far_kernel, 0),
        (place, dkv_far, held_kv, own_half),
        halves[:1],
        flops=2 * 128 * 256 * 1024,
        traffic=1 << 20,
    )
    input_grad = add(own_half, got_half).astype(BF16)
    return input_grad, dk, dv


def solution(mesh):
    split = Mesh(mesh.devices.reshape(8, 4, 2, 2, 2), ("z", "y", "xh", "xl", "core"))
    ctx, tp = ("z", "y", "xh"), ("xl", "core")
    in_specs = (
        P(ctx, tp),
        P(ctx, tp),
        P(None, tp),
        P(None, tp),
        P(None, tp),
        P(tp, None),
        P(),
    )
    out_specs = (P(ctx, tp), P(ctx, tp), P(ctx, tp))
    return jax.shard_map(
        local, mesh=split, in_specs=in_specs, out_specs=out_specs, check_vma=False
    )
```

```python
import functools

import jax
import jax.numpy as jnp
from jax import lax
from jax.experimental import pallas as pl
from jax.experimental.pallas import tpu as pltpu
from jax.sharding import Mesh
from jax.sharding import PartitionSpec as P

HEAD = 128
FACTOR = HEAD**-0.5
LOG2E = 1.4426950408889634
SCALE2 = FACTOR * LOG2E
NEG_FILL = -1e30
LOWEST_TOP = -1e29
BLOCK = 128
HEADS = 4
ROWS = HEADS * BLOCK
CHUNK = 2 * BLOCK
FAR_FLOPS = 10_000_000_000
STEP = 512
NEAR_FLOPS = 2 * 128 * 2048 * 512
STAT_FLOPS = 4 * 2048 * 2048 * 128
GRAD_FLOPS = 10 * 2048 * 2048 * 128
VMEM_LIMIT = 20 * 1024 * 1024
BF16 = jnp.bfloat16
F32 = jnp.float32


def shifted(size, step):
    return [(i, (i + step) % size) for i in range(size)]


def contract_last(left, right):
    return lax.dot_general(
        left, right, (((1,), (1,)), ((), ())), preferred_element_type=F32
    )


def matmul(left, right):
    return jnp.dot(left, right, preferred_element_type=F32)


PAIR = 2048


def near_kernel(
    place, x0, x1, g0, g1, wq, wk, wv, wo,
    x_half, g_half, far_q, far_k, far_v, far_o,
    near_q, near_k, near_v, near_o, g_buf, sems,
):
    xl, core = place[3], place[4]
    near = pl.ds(pl.multiple_of(xl * PAIR, PAIR), PAIR)
    far = pl.ds(pl.multiple_of((1 - xl) * PAIR, PAIR), PAIR)
    copies = []
    for rows, targets in (
        (near, (near_q, near_k, near_v, near_o)),
        (far, (far_q, far_k, far_v, far_o)),
    ):
        for source, target in zip((wq, wk, wv, wo), targets):
            part = source.at[:, rows] if source is wo else source.at[rows, :]
            copies.append(pltpu.make_async_copy(part, target, sems.at[len(copies)]))
    for copy in copies:
        copy.start()
    own, other = core_halves(core)
    for copy, weight, low, high in (
        (copies[0], near_q, 256, 768),
        (copies[1], near_k, 0, 128),
        (copies[2], near_v, 128, 256),
    ):
        copy.wait()
        x_half[:, low:high] = matmul(x0[...], weight[own, :]) + matmul(x1[...], weight[other, :])
    copies[3].wait()
    g_buf[...] = contract_last(g0[...], near_o[:, own]) + contract_last(g1[...], near_o[:, other])
    copies.append(pltpu.make_async_copy(g_buf, g_half, sems.at[8]))
    copies[8].start()
    for copy in copies[4:]:
        copy.wait()


def core_halves(core):
    return [pl.ds(pl.multiple_of(c * 1024, 1024), 1024) for c in (core, 1 - core)]


def far_inputs_kernel(place, x2, x3, wq, wk, wv, x_half, kv, q, kv_buf, q_buf, sems):
    own, other = core_halves(place[4])

    def product(weight, low, high):
        return (
            x_half[:, low:high]
            + matmul(x2[...], weight[own, :])
            + matmul(x3[...], weight[other, :])
        ).astype(BF16)

    pair = jnp.concatenate([product(wk, 0, 128), product(wv, 128, 256)], axis=1)
    for i in range(4):
        kv_buf[i] = pair
    copies = [
        pltpu.make_async_copy(kv_buf, kv.at[pl.ds(4 * i, 4)], sems.at[i]) for i in range(4)
    ]
    for copy in copies:
        copy.start()
    q_buf[...] = product(wq, 256, 768)
    copies.append(pltpu.make_async_copy(q_buf, q, sems.at[4]))
    copies[4].start()
    for copy in copies:
        copy.wait()


def far_grads_kernel(place, g2, g3, wo, g_half, q, out, g_buf, out_buf, sems):
    own, other = core_halves(place[4])
    fetch_g = pltpu.make_async_copy(g_half, g_buf, sems.at[0])
    fetch_q = pltpu.make_async_copy(q, out_buf.at[:, :ROWS], sems.at[1])
    fetch_g.start()
    fetch_q.start()
    far = contract_last(g2[...], wo[:, own]) + contract_last(g3[...], wo[:, other])
    fetch_g.wait()
    out_buf[:, ROWS:] = (g_buf[...] + far).astype(BF16)
    fetch_q.wait()
    store = pltpu.make_async_copy(out_buf, out, sems.at[2])
    store.start()
    store.wait()


def whole_call(
    kernel, operands, outs, scratch=(), hbm=(), hbm_outs=(), flops=0, traffic=0, exps=0
):
    vmem = pl.BlockSpec(memory_space=pltpu.VMEM)
    operands = list(operands)
    in_specs = [vmem] * len(operands)
    in_specs[0] = pl.BlockSpec(memory_space=pltpu.SMEM)
    for i in hbm:
        in_specs[i] = pl.BlockSpec(memory_space=pltpu.HBM)
        operands[i] = pltpu.with_memory_space_constraint(operands[i], pltpu.HBM)
    return pl.pallas_call(
        kernel,
        in_specs=in_specs,
        out_specs=[
            pl.BlockSpec(memory_space=pltpu.HBM) if i in hbm_outs else vmem
            for i in range(len(outs))
        ],
        out_shape=[
            pltpu.HBM(out.shape, out.dtype) if i in hbm_outs else out
            for i, out in enumerate(outs)
        ],
        scratch_shapes=list(scratch),
        compiler_params=pltpu.CompilerParams(vmem_limit_bytes=VMEM_LIMIT),
        cost_estimate=pl.CostEstimate(flops=flops, bytes_accessed=traffic, transcendentals=exps),
    )(*operands)


def stack_heads(ref, first):
    return jnp.concatenate(
        [ref[:, first + h * HEAD : first + (h + 1) * HEAD] for h in range(HEADS)], axis=0
    )


def visible(times, key_block, query_block):
    keys = jnp.broadcast_to(times[pl.ds(key_block, 1), :], (BLOCK, BLOCK)).T
    return jnp.where(keys <= times[pl.ds(query_block, 1), :], 0.0, NEG_FILL)


def stack_kernel(
    place, times_hbm, qd0, qd1, qd2, qd3, wk, wv,
    q_rows, g_rows, bias, far_kv, times, own, weights, sems,
):
    packs = []
    rows = pl.ds(pl.multiple_of((1 - place[3]) * PAIR, PAIR), PAIR)
    for k, weight in enumerate((wk, wv)):
        held = weights.at[k]
        fetched = pltpu.make_async_copy(weight.at[rows, :], held, sems.at[2 + 2 * k])
        packs.append((fetched, pltpu.make_async_copy(held, far_kv.at[k], sems.at[3 + 2 * k])))
    for fetched, _ in packs:
        fetched.start()
    copies = [
        pltpu.make_async_copy(qd0, own, sems.at[0]),
        pltpu.make_async_copy(times_hbm, times, sems.at[1]),
    ]
    for copy in copies:
        copy.start()
    for s, qd in ((1, qd1), (2, qd2), (3, qd3), (0, own)):
        if s == 0:
            copies[0].wait()
        q_rows[s * ROWS : (s + 1) * ROWS, :] = stack_heads(qd, 0)
        g_rows[s * ROWS : (s + 1) * ROWS, :] = stack_heads(qd, 512)
    for fetched, stored in packs:
        fetched.wait()
        stored.start()
    copies[1].wait()
    z, y, xh = place[0], place[1], place[2]
    for s in range(4):
        cols = slice(s * BLOCK, (s + 1) * BLOCK)
        query_block = 8 * z + 2 * ((y - s + 4) % 4) + xh
        for h in range(2):
            key_block = 8 * z + 2 * y + h
            bias[h * BLOCK : (h + 1) * BLOCK, cols] = visible(times, key_block, query_block)
    bias[2 * BLOCK :, :BLOCK] = visible(times, 8 * jnp.minimum(z + 1, 7), 8 * z + 7)
    bias[2 * BLOCK :, BLOCK:] = jnp.full((BLOCK, 3 * BLOCK), NEG_FILL, F32)
    for _, stored in packs:
        stored.wait()


def for_tiles(place, bias, tile, done):
    z, y, xh = place[0], place[1], place[2]

    def masked(part, s):
        return jnp.concatenate([bias[part, s * BLOCK : (s + 1) * BLOCK]] * HEADS, axis=1)

    for s in range(4):
        first = pl.multiple_of(z * CHUNK, CHUNK)
        tile(first, CHUNK, s * ROWS, ROWS, masked(slice(0, CHUNK), s))

    def past(first, keys):
        tile(pl.multiple_of(first, CHUNK), keys, 0, 4 * ROWS, None)

    def some(i, carry):
        past(i * STEP, STEP)
        done(i)
        return carry

    lax.fori_loop(0, z // 2, some, 0)

    @pl.when(z % 2 == 1)
    def _():
        past((z - 1) * CHUNK, CHUNK)

    @pl.when((z < 7) & (y == 0) & (xh == 1))
    def _():
        first = pl.multiple_of((z + 1) * CHUNK, CHUNK)
        tile(first, BLOCK, ROWS, ROWS, masked(slice(CHUNK, CHUNK + BLOCK), 0))


def stats_kernel(place, kv, q_rows, g_rows, bias, out):
    def tile(first, count, row, rows, hidden):
        cols = slice(row, row + rows)
        keys = kv[pl.ds(first, count), :HEAD]
        values = kv[pl.ds(first, count), HEAD:]
        scores = contract_last(keys, q_rows[cols, :])
        first_visit = hidden is not None and count == CHUNK
        if hidden is not None:
            scores = scores + hidden
        top = jnp.maximum(jnp.max(scores, axis=0, keepdims=True) * SCALE2, LOWEST_TOP)
        if not first_visit:
            old = out[0:1, cols]
            top = jnp.maximum(old, top)
        prob = jnp.exp2(scores * SCALE2 - top)
        prob_grad = contract_last(values, g_rows[cols, :])
        norm = jnp.sum(prob, axis=0, keepdims=True)
        dot = jnp.sum(prob * prob_grad, axis=0, keepdims=True)
        if not first_visit:
            shrink = jnp.exp2(old - top)
            norm += out[1:2, cols] * shrink
            dot += out[2:3, cols] * shrink
        out[0:1, cols] = top
        out[1:2, cols] = norm
        out[2:3, cols] = dot

    out[3:4, :] = jnp.zeros((1, 4 * ROWS), F32)
    for_tiles(place, bias, tile, lambda i: None)


def stats(place, kv, rows):
    (out,) = whole_call(
        stats_kernel,
        (place, kv, *rows),
        [jax.ShapeDtypeStruct((4, 4 * ROWS), F32)],
        flops=STAT_FLOPS,
        traffic=2 << 20,
    )
    return out


def grads_kernel(
    place, kv, q_rows, g_rows, bias, st0, st1, st2, st3,
    dkv, dq0, dq1, dq2, dq3,
    sums, q_sum, row_stats, dkv_buf, dq_buf, out_sems,
):
    z = place[0]

    def clear(i, carry):
        dkv_buf[i] = jnp.zeros((BLOCK, 2 * HEAD), BF16)
        return carry

    lax.fori_loop(2 * z + 2, 16, clear, 0)
    for s in range(4):
        cols = slice(s * ROWS, (s + 1) * ROWS)
        tops, norms, dots = [], [], []
        for k, st in enumerate((st0, st1, st2, st3)):
            first = ((s - k) % 4) * ROWS
            tops.append(st[0:1, first : first + ROWS])
            norms.append(st[1:2, first : first + ROWS])
            dots.append(st[2:3, first : first + ROWS])
        top = functools.reduce(jnp.maximum, tops)
        scales = [jnp.exp2(t - top) for t in tops]
        norm = sum(n * f for n, f in zip(norms, scales))
        row_stats[0:1, cols] = top + jnp.log2(norm)
        row_stats[1:2, cols] = sum(d * f for d, f in zip(dots, scales)) / norm

    def tile(first, count, row, rows, hidden):
        cols = slice(row, row + rows)
        keys = kv[pl.ds(first, count), :HEAD]
        values = kv[pl.ds(first, count), HEAD:]
        q, g = q_rows[cols, :], g_rows[cols, :]
        scores = contract_last(keys, q) * SCALE2
        if hidden is not None:
            scores = scores + hidden
        prob = jnp.exp2(scores - row_stats[0:1, cols])
        prob_grad = contract_last(values, g)
        score_grad = (prob * (prob_grad - row_stats[1:2, cols])).astype(BF16)
        dk = matmul(score_grad, q)
        dv = matmul(prob.astype(BF16), g)
        dq = lax.dot_general(
            keys, score_grad, (((0,), (0,)), ((), ())), preferred_element_type=F32
        )
        block = first // BLOCK
        if hidden is not None and count == CHUNK:
            q_sum[:, cols] = dq
            if row:
                dk += sums[:, :HEAD]
                dv += sums[:, HEAD:]
            sums[:, :HEAD] = dk
            sums[:, HEAD:] = dv
            if row < 3 * ROWS:
                return
        else:
            q_sum[:, cols] += dq
        for i in range(count // BLOCK):
            part = slice(i * BLOCK, (i + 1) * BLOCK)
            dkv_buf[block + i, :, :HEAD] = dk[part, :].astype(BF16)
            dkv_buf[block + i, :, HEAD:] = dv[part, :].astype(BF16)

    def send(i):
        part = pl.ds(4 * i, 4)
        return pltpu.make_async_copy(dkv_buf.at[part], dkv.at[part], out_sems.at[i])

    for_tiles(place, bias, tile, lambda i: send(i).start())
    for i in range(4):

        @pl.when(i >= z // 2)
        def _():
            send(i).start()

    outs = []
    for s, dq in enumerate((dq0, dq1, dq2, dq3)):
        for h in range(HEADS):
            part = q_sum[:, s * ROWS + h * HEAD : s * ROWS + (h + 1) * HEAD]
            dq_buf[s, :, h * HEAD : (h + 1) * HEAD] = (part.T * FACTOR).astype(BF16)
        outs.append(pltpu.make_async_copy(dq_buf.at[s], dq, out_sems.at[4 + s]))
        outs[-1].start()
    for i in range(4):
        send(i).wait()
    for copy in outs:
        copy.wait()


def grads(place, kv, rows, gathered):
    return whole_call(
        grads_kernel,
        (place, kv, *rows, *gathered),
        [jax.ShapeDtypeStruct((16, BLOCK, 2 * HEAD), BF16)]
        + [jax.ShapeDtypeStruct((BLOCK, ROWS), BF16)] * 4,
        [
            pltpu.VMEM((CHUNK, 2 * HEAD), F32),
            pltpu.VMEM((HEAD, 4 * ROWS), F32),
            pltpu.VMEM((8, 4 * ROWS), F32),
            pltpu.VMEM((16, BLOCK, 2 * HEAD), BF16),
            pltpu.VMEM((4, BLOCK, ROWS), BF16),
            pltpu.SemaphoreType.DMA((8,)),
        ],
        hbm_outs=(0, 1, 2, 3, 4),
        flops=GRAD_FLOPS,
        traffic=4 << 20,
    )


def feature_rows(place, flip):
    first = (2 * place[3] + place[4]) ^ flip
    return pl.ds(pl.multiple_of(first * 1024, 1024), 1024)


def query_far_kernel(place, dq0, dq1, dq2, dq3, wq, far0, far1, total, held, sems):
    copies = [
        pltpu.make_async_copy(wq.at[feature_rows(place, flip), :], held.at[i], sems.at[i])
        for i, flip in enumerate((3, 2))
    ]
    for copy in copies:
        copy.start()
    parts = [d[...].astype(F32) for d in (dq0, dq1, dq2, dq3)]
    total[...] = (parts[0] + parts[1] + parts[2] + parts[3]).astype(BF16)
    for copy, block, out in zip(copies, (0, 1), (far0, far1)):
        copy.wait()
        out[...] = contract_last(total[...], held[block]).astype(out.dtype)


def query_near_kernel(place, total, wq, wk, wv, got_kv, near1, near0, out_kv, held, sems):
    copies = [
        pltpu.make_async_copy(wq.at[feature_rows(place, flip), :], held.at[i], sems.at[i])
        for i, flip in enumerate((1, 0))
    ]
    rows = pl.ds(pl.multiple_of(place[3] * PAIR, PAIR), PAIR)
    sources = (wk.at[rows, :], wv.at[rows, :], got_kv.at[0], got_kv.at[1])
    for i, source in enumerate(sources):
        low = (i % 2) * HEAD
        target = out_kv.at[i // 2, :, low : low + HEAD]
        copies.append(pltpu.make_async_copy(source, target, sems.at[2 + i]))
    for copy in copies:
        copy.start()
    for copy, block, out in zip(copies, (0, 1), (near1, near0)):
        copy.wait()
        out[...] = contract_last(total[...], held[block]).astype(out.dtype)
    for copy in copies[2:]:
        copy.wait()


def key_sum_kernel(place, parts, dk, dv, dkv):
    total = parts[0].astype(F32)
    for i in range(1, 16):
        total = total + parts[i].astype(F32)
    dk[...] = (total[:, :HEAD] * FACTOR).astype(BF16)
    dv[...] = total[:, HEAD:].astype(BF16)
    dkv[:, :HEAD] = dk[...]
    dkv[:, HEAD:] = dv[...]


def key_near_kernel(place, dkv, weights, queries, far_queries, own, other):
    mine, siblings = core_halves(place[4])
    total = queries[...].astype(F32) + far_queries[...].astype(F32)
    own[...] = total + contract_last(dkv[...], weights[0, mine, :])
    other[...] = contract_last(dkv[...], weights[0, siblings, :])


def key_far_kernel(flip, place, dkv, weights, before, out):
    rows = core_halves(place[4])[flip]
    out[...] = (before[...] + contract_last(dkv[...], weights[1, rows, :])).astype(out.dtype)


def local(inputs, out_grad, w_query, key_weight, value_weight, w_output, times):
    axes = ("z", "y", "xh", "xl", "core")
    place = jnp.stack([lax.axis_index(name) for name in axes]).astype(jnp.int32)
    times2d = times.reshape(64, BLOCK)
    swap = shifted(2, 1)

    def to_core(value):
        return lax.ppermute(value, "core", swap)

    def to_xl(value):
        return lax.ppermute(value, "xl", swap)

    def shape(*dims, kind=BF16):
        return jax.ShapeDtypeStruct(dims, kind)

    x2, g2 = to_xl(inputs), to_xl(out_grad)
    x1, g1 = to_core(inputs), to_core(out_grad)
    held = [
        shape(PAIR, ROWS), shape(PAIR, HEAD), shape(PAIR, HEAD), shape(ROWS, PAIR)
    ]
    x_half, g_half, far_q, far_k, far_v, far_o = whole_call(
        near_kernel,
        (place, inputs, x1, out_grad, g1, w_query, key_weight, value_weight, w_output),
        [shape(BLOCK, 768, kind=F32), shape(BLOCK, ROWS, kind=F32)] + held,
        [pltpu.VMEM(h.shape, BF16) for h in held]
        + [pltpu.VMEM((BLOCK, ROWS), F32), pltpu.SemaphoreType.DMA((9,))],
        hbm=(5, 6, 7, 8),
        hbm_outs=(1,),
        flops=2 * 128 * 2048 * 1280,
        traffic=10 << 20,
    )
    x2, x_half, g_half = lax.optimization_barrier((x2, x_half, g_half))
    x3 = to_core(x2)
    kv_own, q_own = whole_call(
        far_inputs_kernel,
        (place, x2, x3, far_q, far_k, far_v, x_half),
        [shape(16, BLOCK, 2 * HEAD), shape(BLOCK, ROWS)],
        [
            pltpu.VMEM((4, BLOCK, 2 * HEAD), BF16),
            pltpu.VMEM((BLOCK, ROWS), BF16),
            pltpu.SemaphoreType.DMA((5,)),
        ],
        hbm_outs=(0, 1),
        flops=2 * 128 * 2048 * 768,
        traffic=4 << 20,
    )
    g2, q_own = lax.optimization_barrier((g2, q_own))
    g3 = to_core(g2)
    (qd_own,) = whole_call(
        far_grads_kernel,
        (place, g2, g3, far_o, g_half, q_own),
        [shape(BLOCK, 1024)],
        [
            pltpu.VMEM((BLOCK, ROWS), F32),
            pltpu.VMEM((BLOCK, 1024), BF16),
            pltpu.SemaphoreType.DMA((3,)),
        ],
        hbm=(4, 5),
        hbm_outs=(0,),
        flops=FAR_FLOPS,
        traffic=3 << 20,
    )
    kv = lax.all_to_all(kv_own, ("z", "xh"), 0, 0, tiled=True).reshape(16 * BLOCK, 2 * HEAD)
    blocks = [qd_own] + [lax.ppermute(qd_own, "y", shifted(4, s)) for s in (1, 2, 3)]

    *rows, far_kv = whole_call(
        stack_kernel,
        (place, times2d, *blocks, key_weight, value_weight),
        [shape(4 * ROWS, HEAD)] * 2
        + [shape(CHUNK + BLOCK, ROWS, kind=F32)]
        + [shape(2, PAIR, HEAD)],
        [
            pltpu.VMEM((64, BLOCK), jnp.int32),
            pltpu.VMEM((BLOCK, 1024), BF16),
            pltpu.VMEM((2, PAIR, HEAD), BF16),
            pltpu.SemaphoreType.DMA((6,)),
        ],
        hbm=(1, 2, 6, 7),
        hbm_outs=(3,),
        traffic=2 << 20,
    )
    got_kv = to_xl(far_kv)
    own_stats = stats(place, kv, rows)
    gathered = [own_stats] + [lax.ppermute(own_stats, "y", shifted(4, s)) for s in (1, 2, 3)]
    dkv, *dqs = grads(place, kv, rows, gathered)

    dkv, got_kv = lax.optimization_barrier((dkv, got_kv))
    dkv_parts = lax.all_to_all(dkv, ("z", "xh"), 0, 0, tiled=True)
    dq_parts = [dqs[0]] + [lax.ppermute(dqs[s], "y", shifted(4, -s)) for s in (1, 2, 3)]

    def add(*values):
        return sum(v.astype(F32) for v in values)

    far0, far1, dq = whole_call(
        query_far_kernel,
        (place, *dq_parts, w_query),
        [shape(BLOCK, 1024)] * 2 + [shape(BLOCK, ROWS)],
        [pltpu.VMEM((2, 1024, ROWS), BF16), pltpu.SemaphoreType.DMA((2,))],
        hbm=(5,),
        flops=2 * 128 * 2048 * 512,
        traffic=2 << 20,
    )
    far_sum = add(far1, to_core(far0)).astype(BF16)
    far_sum, dq = lax.optimization_barrier((far_sum, dq))
    far_queries = to_xl(far_sum)
    near1, near0, held_kv = whole_call(
        query_near_kernel,
        (place, dq, w_query, key_weight, value_weight, got_kv),
        [shape(BLOCK, 1024)] * 2 + [shape(2, PAIR, 2 * HEAD)],
        [pltpu.VMEM((2, 1024, ROWS), BF16), pltpu.SemaphoreType.DMA((6,))],
        hbm=(2, 3, 4, 5),
        flops=NEAR_FLOPS,
        traffic=4 << 20,
    )
    near_queries = add(near0, to_core(near1)).astype(BF16)
    dkv_parts, near_queries = lax.optimization_barrier((dkv_parts, near_queries))

    dk, dv, dkv_own = whole_call(
        key_sum_kernel,
        (place, dkv_parts),
        [shape(BLOCK, HEAD)] * 2 + [shape(BLOCK, 2 * HEAD)],
        traffic=2 << 20,
    )
    dkv_far = to_xl(dkv_own)
    halves = [shape(BLOCK, 1024, kind=F32)] * 2
    own_half, other_half = whole_call(
        key_near_kernel,
        (place, dkv_own, held_kv, near_queries, far_queries),
        halves,
        flops=2 * 128 * 256 * 2048,
        traffic=2 << 20,
    )
    (other_half,) = whole_call(
        functools.partial(key_far_kernel, 1),
        (place, dkv_far, held_kv, other_half),
        [shape(BLOCK, 1024)],
        flops=2 * 128 * 256 * 1024,
        traffic=1 << 20,
    )
    got_half = to_core(other_half)
    (own_half,) = whole_call(
        functools.partial(key_far_kernel, 0),
        (place, dkv_far, held_kv, own_half),
        halves[:1],
        flops=2 * 128 * 256 * 1024,
        traffic=1 << 20,
    )
    input_grad = add(own_half, got_half).astype(BF16)
    return input_grad, dk, dv


def solution(mesh):
    split = Mesh(mesh.devices.reshape(8, 4, 2, 2, 2), ("z", "y", "xh", "xl", "core"))
    ctx, tp = ("z", "y", "xh"), ("xl", "core")
    in_specs = (
        P(ctx, tp),
        P(ctx, tp),
        P(None, tp),
        P(None, tp),
        P(None, tp),
        P(tp, None),
        P(),
    )
    out_specs = (P(ctx, tp), P(ctx, tp), P(ctx, tp))
    return jax.shard_map(
        local, mesh=split, in_specs=in_specs, out_specs=out_specs, check_vma=False
    )
```

```python
import functools

import jax
import jax.numpy as jnp
from jax import lax
from jax.experimental import pallas as pl
from jax.experimental.pallas import tpu as pltpu
from jax.sharding import Mesh
from jax.sharding import PartitionSpec as P

HEAD = 128
FACTOR = HEAD**-0.5
LOG2E = 1.4426950408889634
SCALE2 = FACTOR * LOG2E
NEG_FILL = -1e30
LOWEST_TOP = -1e29
BLOCK = 128
HEADS = 4
ROWS = HEADS * BLOCK
CHUNK = 2 * BLOCK
FAR_FLOPS = 10_000_000_000
STEP = 512
NEAR_FLOPS = 2 * 128 * 2048 * 512
STAT_FLOPS = 4 * 2048 * 2048 * 128
GRAD_FLOPS = 10 * 2048 * 2048 * 128
VMEM_LIMIT = 20 * 1024 * 1024
BF16 = jnp.bfloat16
F32 = jnp.float32


def shifted(size, step):
    return [(i, (i + step) % size) for i in range(size)]


def contract_last(left, right):
    return lax.dot_general(
        left, right, (((1,), (1,)), ((), ())), preferred_element_type=F32
    )


def matmul(left, right):
    return jnp.dot(left, right, preferred_element_type=F32)


PAIR = 2048


def near_kernel(
    place, x0, x1, g0, g1, wq, wk, wv, wo,
    x_half, g_half, far_q, far_kv, far_o,
    near_q, near_k, near_v, near_o, g_buf, sems,
):
    xl, core = place[3], place[4]
    near = pl.ds(pl.multiple_of(xl * PAIR, PAIR), PAIR)
    far = pl.ds(pl.multiple_of((1 - xl) * PAIR, PAIR), PAIR)
    copies = []
    for rows, targets in (
        (near, (near_q, near_k, near_v, near_o)),
        (far, (far_q, far_kv.at[:, :HEAD], far_kv.at[:, HEAD:], far_o)),
    ):
        for source, target in zip((wq, wk, wv, wo), targets):
            part = source.at[:, rows] if source is wo else source.at[rows, :]
            copies.append(pltpu.make_async_copy(part, target, sems.at[len(copies)]))
    for copy in copies:
        copy.start()
    own, other = core_halves(core)
    for copy, weight, low, high in (
        (copies[0], near_q, 256, 768),
        (copies[1], near_k, 0, 128),
        (copies[2], near_v, 128, 256),
    ):
        copy.wait()
        x_half[:, low:high] = matmul(x0[...], weight[own, :]) + matmul(x1[...], weight[other, :])
    copies[3].wait()
    g_buf[...] = contract_last(g0[...], near_o[:, own]) + contract_last(g1[...], near_o[:, other])
    copies.append(pltpu.make_async_copy(g_buf, g_half, sems.at[8]))
    copies[8].start()
    for copy in copies[4:]:
        copy.wait()


def core_halves(core):
    return [pl.ds(pl.multiple_of(c * 1024, 1024), 1024) for c in (core, 1 - core)]


def far_inputs_kernel(place, x2, x3, wq, wkv, x_half, kv, q, kv_buf, q_buf, sems):
    own, other = core_halves(place[4])

    def product(weight, low, high):
        return (
            x_half[:, low:high]
            + matmul(x2[...], weight[own, :])
            + matmul(x3[...], weight[other, :])
        ).astype(BF16)

    pair = product(wkv, 0, 256)
    for i in range(4):
        kv_buf[i] = pair
    copies = [
        pltpu.make_async_copy(kv_buf, kv.at[pl.ds(4 * i, 4)], sems.at[i]) for i in range(4)
    ]
    for copy in copies:
        copy.start()
    q_buf[...] = product(wq, 256, 768)
    copies.append(pltpu.make_async_copy(q_buf, q, sems.at[4]))
    copies[4].start()
    for copy in copies:
        copy.wait()


def far_grads_kernel(place, g2, g3, wo, g_half, q, out, g_buf, out_buf, sems):
    own, other = core_halves(place[4])
    fetch_g = pltpu.make_async_copy(g_half, g_buf, sems.at[0])
    fetch_q = pltpu.make_async_copy(q, out_buf.at[:, :ROWS], sems.at[1])
    fetch_g.start()
    fetch_q.start()
    far = contract_last(g2[...], wo[:, own]) + contract_last(g3[...], wo[:, other])
    fetch_g.wait()
    out_buf[:, ROWS:] = (g_buf[...] + far).astype(BF16)
    fetch_q.wait()
    store = pltpu.make_async_copy(out_buf, out, sems.at[2])
    store.start()
    store.wait()


def whole_call(
    kernel, operands, outs, scratch=(), hbm=(), hbm_outs=(), flops=0, traffic=0, exps=0
):
    vmem = pl.BlockSpec(memory_space=pltpu.VMEM)
    operands = list(operands)
    in_specs = [vmem] * len(operands)
    in_specs[0] = pl.BlockSpec(memory_space=pltpu.SMEM)
    for i in hbm:
        in_specs[i] = pl.BlockSpec(memory_space=pltpu.HBM)
        operands[i] = pltpu.with_memory_space_constraint(operands[i], pltpu.HBM)
    return pl.pallas_call(
        kernel,
        in_specs=in_specs,
        out_specs=[
            pl.BlockSpec(memory_space=pltpu.HBM) if i in hbm_outs else vmem
            for i in range(len(outs))
        ],
        out_shape=[
            pltpu.HBM(out.shape, out.dtype) if i in hbm_outs else out
            for i, out in enumerate(outs)
        ],
        scratch_shapes=list(scratch),
        compiler_params=pltpu.CompilerParams(vmem_limit_bytes=VMEM_LIMIT),
        cost_estimate=pl.CostEstimate(flops=flops, bytes_accessed=traffic, transcendentals=exps),
    )(*operands)


def stack_heads(ref, first):
    return jnp.concatenate(
        [ref[:, first + h * HEAD : first + (h + 1) * HEAD] for h in range(HEADS)], axis=0
    )


def visible(times, key_block, query_block):
    keys = jnp.broadcast_to(times[pl.ds(key_block, 1), :], (BLOCK, BLOCK)).T
    return jnp.where(keys <= times[pl.ds(query_block, 1), :], 0.0, NEG_FILL)


def stack_kernel(
    place, times_hbm, qd0, qd1, qd2, qd3, wk, wv,
    q_rows, g_rows, bias, far_kv, times, own, weights, sems,
):
    packs = []
    rows = pl.ds(pl.multiple_of((1 - place[3]) * PAIR, PAIR), PAIR)
    for k, weight in enumerate((wk, wv)):
        held = weights.at[k]
        fetched = pltpu.make_async_copy(weight.at[rows, :], held, sems.at[2 + 2 * k])
        packs.append((fetched, pltpu.make_async_copy(held, far_kv.at[k], sems.at[3 + 2 * k])))
    for fetched, _ in packs:
        fetched.start()
    copies = [
        pltpu.make_async_copy(qd0, own, sems.at[0]),
        pltpu.make_async_copy(times_hbm, times, sems.at[1]),
    ]
    for copy in copies:
        copy.start()
    for s, qd in ((1, qd1), (2, qd2), (3, qd3), (0, own)):
        if s == 0:
            copies[0].wait()
        q_rows[s * ROWS : (s + 1) * ROWS, :] = stack_heads(qd, 0)
        g_rows[s * ROWS : (s + 1) * ROWS, :] = stack_heads(qd, 512)
    for fetched, stored in packs:
        fetched.wait()
        stored.start()
    copies[1].wait()
    z, y, xh = place[0], place[1], place[2]
    for s in range(4):
        cols = slice(s * BLOCK, (s + 1) * BLOCK)
        query_block = 8 * z + 2 * ((y - s + 4) % 4) + xh
        for h in range(2):
            key_block = 8 * z + 2 * y + h
            bias[h * BLOCK : (h + 1) * BLOCK, cols] = visible(times, key_block, query_block)
    bias[2 * BLOCK :, :BLOCK] = visible(times, 8 * jnp.minimum(z + 1, 7), 8 * z + 7)
    bias[2 * BLOCK :, BLOCK:] = jnp.full((BLOCK, 3 * BLOCK), NEG_FILL, F32)
    for _, stored in packs:
        stored.wait()


def for_tiles(place, bias, tile, done):
    z, y, xh = place[0], place[1], place[2]

    def masked(part, s):
        return jnp.concatenate([bias[part, s * BLOCK : (s + 1) * BLOCK]] * HEADS, axis=1)

    for s in range(4):
        first = pl.multiple_of(z * CHUNK, CHUNK)
        tile(first, CHUNK, s * ROWS, ROWS, masked(slice(0, CHUNK), s))

    def past(first, keys):
        tile(pl.multiple_of(first, CHUNK), keys, 0, 4 * ROWS, None)

    def some(i, carry):
        past(i * STEP, STEP)
        done(i)
        return carry

    lax.fori_loop(0, z // 2, some, 0)

    @pl.when(z % 2 == 1)
    def _():
        past((z - 1) * CHUNK, CHUNK)

    @pl.when((z < 7) & (y == 0) & (xh == 1))
    def _():
        first = pl.multiple_of((z + 1) * CHUNK, CHUNK)
        tile(first, BLOCK, ROWS, ROWS, masked(slice(CHUNK, CHUNK + BLOCK), 0))


def stats_kernel(place, kv, q_rows, g_rows, bias, out):
    def tile(first, count, row, rows, hidden):
        cols = slice(row, row + rows)
        keys = kv[pl.ds(first, count), :HEAD]
        values = kv[pl.ds(first, count), HEAD:]
        scores = contract_last(keys, q_rows[cols, :])
        first_visit = hidden is not None and count == CHUNK
        if hidden is not None:
            scores = scores + hidden
        top = jnp.maximum(jnp.max(scores, axis=0, keepdims=True) * SCALE2, LOWEST_TOP)
        if not first_visit:
            old = out[0:1, cols]
            top = jnp.maximum(old, top)
        prob = jnp.exp2(scores * SCALE2 - top)
        prob_grad = contract_last(values, g_rows[cols, :])
        norm = jnp.sum(prob, axis=0, keepdims=True)
        dot = jnp.sum(prob * prob_grad, axis=0, keepdims=True)
        if not first_visit:
            shrink = jnp.exp2(old - top)
            norm += out[1:2, cols] * shrink
            dot += out[2:3, cols] * shrink
        out[0:1, cols] = top
        out[1:2, cols] = norm
        out[2:3, cols] = dot

    out[3:4, :] = jnp.zeros((1, 4 * ROWS), F32)
    for_tiles(place, bias, tile, lambda i: None)


def stats(place, kv, rows):
    (out,) = whole_call(
        stats_kernel,
        (place, kv, *rows),
        [jax.ShapeDtypeStruct((4, 4 * ROWS), F32)],
        flops=STAT_FLOPS,
        traffic=2 << 20,
    )
    return out


def grads_kernel(
    place, kv, q_rows, g_rows, bias, st0, st1, st2, st3,
    dkv, dq0, dq1, dq2, dq3,
    sums, q_sum, row_stats, dkv_buf, dq_buf, out_sems,
):
    z = place[0]

    def clear(i, carry):
        dkv_buf[i] = jnp.zeros((BLOCK, 2 * HEAD), BF16)
        return carry

    lax.fori_loop(2 * z + 2, 16, clear, 0)
    for s in range(4):
        cols = slice(s * ROWS, (s + 1) * ROWS)
        tops, norms, dots = [], [], []
        for k, st in enumerate((st0, st1, st2, st3)):
            first = ((s - k) % 4) * ROWS
            tops.append(st[0:1, first : first + ROWS])
            norms.append(st[1:2, first : first + ROWS])
            dots.append(st[2:3, first : first + ROWS])
        top = functools.reduce(jnp.maximum, tops)
        scales = [jnp.exp2(t - top) for t in tops]
        norm = sum(n * f for n, f in zip(norms, scales))
        row_stats[0:1, cols] = top + jnp.log2(norm)
        row_stats[1:2, cols] = sum(d * f for d, f in zip(dots, scales)) / norm

    def tile(first, count, row, rows, hidden):
        cols = slice(row, row + rows)
        keys = kv[pl.ds(first, count), :HEAD]
        values = kv[pl.ds(first, count), HEAD:]
        q, g = q_rows[cols, :], g_rows[cols, :]
        scores = contract_last(keys, q) * SCALE2
        if hidden is not None:
            scores = scores + hidden
        prob = jnp.exp2(scores - row_stats[0:1, cols])
        prob_grad = contract_last(values, g)
        score_grad = (prob * (prob_grad - row_stats[1:2, cols])).astype(BF16)
        dk = matmul(score_grad, q)
        dv = matmul(prob.astype(BF16), g)
        dq = lax.dot_general(
            keys, score_grad, (((0,), (0,)), ((), ())), preferred_element_type=F32
        )
        block = first // BLOCK
        if hidden is not None and count == CHUNK:
            q_sum[:, cols] = dq
            if row:
                dk += sums[:, :HEAD]
                dv += sums[:, HEAD:]
            sums[:, :HEAD] = dk
            sums[:, HEAD:] = dv
            if row < 3 * ROWS:
                return
        else:
            q_sum[:, cols] += dq
        for i in range(count // BLOCK):
            part = slice(i * BLOCK, (i + 1) * BLOCK)
            dkv_buf[block + i, :, :HEAD] = dk[part, :].astype(BF16)
            dkv_buf[block + i, :, HEAD:] = dv[part, :].astype(BF16)

    def send(i):
        part = pl.ds(4 * i, 4)
        return pltpu.make_async_copy(dkv_buf.at[part], dkv.at[part], out_sems.at[i])

    for_tiles(place, bias, tile, lambda i: send(i).start())
    for i in range(4):

        @pl.when(i >= z // 2)
        def _():
            send(i).start()

    outs = []
    for s, dq in enumerate((dq0, dq1, dq2, dq3)):
        for h in range(HEADS):
            part = q_sum[:, s * ROWS + h * HEAD : s * ROWS + (h + 1) * HEAD]
            dq_buf[s, :, h * HEAD : (h + 1) * HEAD] = (part.T * FACTOR).astype(BF16)
        outs.append(pltpu.make_async_copy(dq_buf.at[s], dq, out_sems.at[4 + s]))
        outs[-1].start()
    for i in range(4):
        send(i).wait()
    for copy in outs:
        copy.wait()


def grads(place, kv, rows, gathered):
    return whole_call(
        grads_kernel,
        (place, kv, *rows, *gathered),
        [jax.ShapeDtypeStruct((16, BLOCK, 2 * HEAD), BF16)]
        + [jax.ShapeDtypeStruct((BLOCK, ROWS), BF16)] * 4,
        [
            pltpu.VMEM((CHUNK, 2 * HEAD), F32),
            pltpu.VMEM((HEAD, 4 * ROWS), F32),
            pltpu.VMEM((8, 4 * ROWS), F32),
            pltpu.VMEM((16, BLOCK, 2 * HEAD), BF16),
            pltpu.VMEM((4, BLOCK, ROWS), BF16),
            pltpu.SemaphoreType.DMA((8,)),
        ],
        hbm_outs=(0, 1, 2, 3, 4),
        flops=GRAD_FLOPS,
        traffic=4 << 20,
    )


def feature_rows(place, flip):
    first = (2 * place[3] + place[4]) ^ flip
    return pl.ds(pl.multiple_of(first * 1024, 1024), 1024)


def query_far_kernel(place, dq0, dq1, dq2, dq3, wq, far0, far1, total, held, sems):
    copies = [
        pltpu.make_async_copy(wq.at[feature_rows(place, flip), :], held.at[i], sems.at[i])
        for i, flip in enumerate((3, 2))
    ]
    for copy in copies:
        copy.start()
    parts = [d[...].astype(F32) for d in (dq0, dq1, dq2, dq3)]
    total[...] = (parts[0] + parts[1] + parts[2] + parts[3]).astype(BF16)
    for copy, block, out in zip(copies, (0, 1), (far0, far1)):
        copy.wait()
        out[...] = contract_last(total[...], held[block]).astype(out.dtype)


def query_near_kernel(place, total, wq, wk, wv, got_kv, near1, near0, out_kv, held, sems):
    copies = [
        pltpu.make_async_copy(wq.at[feature_rows(place, flip), :], held.at[i], sems.at[i])
        for i, flip in enumerate((1, 0))
    ]
    rows = pl.ds(pl.multiple_of(place[3] * PAIR, PAIR), PAIR)
    sources = (wk.at[rows, :], wv.at[rows, :], got_kv.at[0], got_kv.at[1])
    for i, source in enumerate(sources):
        low = (i % 2) * HEAD
        target = out_kv.at[i // 2, :, low : low + HEAD]
        copies.append(pltpu.make_async_copy(source, target, sems.at[2 + i]))
    for copy in copies:
        copy.start()
    for copy, block, out in zip(copies, (0, 1), (near1, near0)):
        copy.wait()
        out[...] = contract_last(total[...], held[block]).astype(out.dtype)
    for copy in copies[2:]:
        copy.wait()


def key_sum_kernel(place, parts, dk, dv, dkv):
    total = parts[0].astype(F32)
    for i in range(1, 16):
        total = total + parts[i].astype(F32)
    dk[...] = (total[:, :HEAD] * FACTOR).astype(BF16)
    dv[...] = total[:, HEAD:].astype(BF16)
    dkv[:, :HEAD] = dk[...]
    dkv[:, HEAD:] = dv[...]


def key_near_kernel(place, dkv, weights, queries, far_queries, own, other):
    mine, siblings = core_halves(place[4])
    total = queries[...].astype(F32) + far_queries[...].astype(F32)
    own[...] = total + contract_last(dkv[...], weights[0, mine, :])
    other[...] = contract_last(dkv[...], weights[0, siblings, :])


def key_far_kernel(flip, place, dkv, weights, before, out):
    rows = core_halves(place[4])[flip]
    out[...] = (before[...] + contract_last(dkv[...], weights[1, rows, :])).astype(out.dtype)


def local(inputs, out_grad, w_query, key_weight, value_weight, w_output, times):
    axes = ("z", "y", "xh", "xl", "core")
    place = jnp.stack([lax.axis_index(name) for name in axes]).astype(jnp.int32)
    times2d = times.reshape(64, BLOCK)
    swap = shifted(2, 1)

    def to_core(value):
        return lax.ppermute(value, "core", swap)

    def to_xl(value):
        return lax.ppermute(value, "xl", swap)

    def shape(*dims, kind=BF16):
        return jax.ShapeDtypeStruct(dims, kind)

    x2, g2 = to_xl(inputs), to_xl(out_grad)
    x1, g1 = to_core(inputs), to_core(out_grad)
    held = [
        shape(PAIR, ROWS), shape(PAIR, HEAD), shape(PAIR, HEAD), shape(ROWS, PAIR)
    ]
    x_half, g_half, far_q, far_kv, far_o = whole_call(
        near_kernel,
        (place, inputs, x1, out_grad, g1, w_query, key_weight, value_weight, w_output),
        [shape(BLOCK, 768, kind=F32), shape(BLOCK, ROWS, kind=F32)]
        + [held[0], shape(PAIR, 2 * HEAD), held[3]],
        [pltpu.VMEM(h.shape, BF16) for h in held]
        + [pltpu.VMEM((BLOCK, ROWS), F32), pltpu.SemaphoreType.DMA((9,))],
        hbm=(5, 6, 7, 8),
        hbm_outs=(1,),
        flops=2 * 128 * 2048 * 1280,
        traffic=10 << 20,
    )
    x2, x_half, g_half = lax.optimization_barrier((x2, x_half, g_half))
    x3 = to_core(x2)
    kv_own, q_own = whole_call(
        far_inputs_kernel,
        (place, x2, x3, far_q, far_kv, x_half),
        [shape(16, BLOCK, 2 * HEAD), shape(BLOCK, ROWS)],
        [
            pltpu.VMEM((4, BLOCK, 2 * HEAD), BF16),
            pltpu.VMEM((BLOCK, ROWS), BF16),
            pltpu.SemaphoreType.DMA((5,)),
        ],
        hbm_outs=(0, 1),
        flops=2 * 128 * 2048 * 768,
        traffic=4 << 20,
    )
    g2, q_own = lax.optimization_barrier((g2, q_own))
    g3 = to_core(g2)
    (qd_own,) = whole_call(
        far_grads_kernel,
        (place, g2, g3, far_o, g_half, q_own),
        [shape(BLOCK, 1024)],
        [
            pltpu.VMEM((BLOCK, ROWS), F32),
            pltpu.VMEM((BLOCK, 1024), BF16),
            pltpu.SemaphoreType.DMA((3,)),
        ],
        hbm=(4, 5),
        hbm_outs=(0,),
        flops=FAR_FLOPS,
        traffic=3 << 20,
    )
    kv = lax.all_to_all(kv_own, ("z", "xh"), 0, 0, tiled=True).reshape(16 * BLOCK, 2 * HEAD)
    blocks = [qd_own] + [lax.ppermute(qd_own, "y", shifted(4, s)) for s in (1, 2, 3)]

    *rows, sent_kv = whole_call(
        stack_kernel,
        (place, times2d, *blocks, key_weight, value_weight),
        [shape(4 * ROWS, HEAD)] * 2
        + [shape(CHUNK + BLOCK, ROWS, kind=F32)]
        + [shape(2, PAIR, HEAD)],
        [
            pltpu.VMEM((64, BLOCK), jnp.int32),
            pltpu.VMEM((BLOCK, 1024), BF16),
            pltpu.VMEM((2, PAIR, HEAD), BF16),
            pltpu.SemaphoreType.DMA((6,)),
        ],
        hbm=(1, 2, 6, 7),
        hbm_outs=(3,),
        traffic=2 << 20,
    )
    got_kv = to_xl(sent_kv)
    own_stats = stats(place, kv, rows)
    gathered = [own_stats] + [lax.ppermute(own_stats, "y", shifted(4, s)) for s in (1, 2, 3)]
    dkv, *dqs = grads(place, kv, rows, gathered)

    dkv, got_kv = lax.optimization_barrier((dkv, got_kv))
    dkv_parts = lax.all_to_all(dkv, ("z", "xh"), 0, 0, tiled=True)
    dq_parts = [dqs[0]] + [lax.ppermute(dqs[s], "y", shifted(4, -s)) for s in (1, 2, 3)]

    def add(*values):
        return sum(v.astype(F32) for v in values)

    far0, far1, dq = whole_call(
        query_far_kernel,
        (place, *dq_parts, w_query),
        [shape(BLOCK, 1024)] * 2 + [shape(BLOCK, ROWS)],
        [pltpu.VMEM((2, 1024, ROWS), BF16), pltpu.SemaphoreType.DMA((2,))],
        hbm=(5,),
        flops=2 * 128 * 2048 * 512,
        traffic=2 << 20,
    )
    far_sum = add(far1, to_core(far0)).astype(BF16)
    far_sum, dq = lax.optimization_barrier((far_sum, dq))
    far_queries = to_xl(far_sum)
    near1, near0, held_kv = whole_call(
        query_near_kernel,
        (place, dq, w_query, key_weight, value_weight, got_kv),
        [shape(BLOCK, 1024)] * 2 + [shape(2, PAIR, 2 * HEAD)],
        [pltpu.VMEM((2, 1024, ROWS), BF16), pltpu.SemaphoreType.DMA((6,))],
        hbm=(2, 3, 4, 5),
        flops=NEAR_FLOPS,
        traffic=4 << 20,
    )
    near_queries = add(near0, to_core(near1)).astype(BF16)
    dkv_parts, near_queries = lax.optimization_barrier((dkv_parts, near_queries))

    dk, dv, dkv_own = whole_call(
        key_sum_kernel,
        (place, dkv_parts),
        [shape(BLOCK, HEAD)] * 2 + [shape(BLOCK, 2 * HEAD)],
        traffic=2 << 20,
    )
    dkv_far = to_xl(dkv_own)
    halves = [shape(BLOCK, 1024, kind=F32)] * 2
    own_half, other_half = whole_call(
        key_near_kernel,
        (place, dkv_own, held_kv, near_queries, far_queries),
        halves,
        flops=2 * 128 * 256 * 2048,
        traffic=2 << 20,
    )
    (other_half,) = whole_call(
        functools.partial(key_far_kernel, 1),
        (place, dkv_far, held_kv, other_half),
        [shape(BLOCK, 1024)],
        flops=2 * 128 * 256 * 1024,
        traffic=1 << 20,
    )
    got_half = to_core(other_half)
    (own_half,) = whole_call(
        functools.partial(key_far_kernel, 0),
        (place, dkv_far, held_kv, own_half),
        halves[:1],
        flops=2 * 128 * 256 * 1024,
        traffic=1 << 20,
    )
    input_grad = add(own_half, got_half).astype(BF16)
    return input_grad, dk, dv


def solution(mesh):
    split = Mesh(mesh.devices.reshape(8, 4, 2, 2, 2), ("z", "y", "xh", "xl", "core"))
    ctx, tp = ("z", "y", "xh"), ("xl", "core")
    in_specs = (
        P(ctx, tp),
        P(ctx, tp),
        P(None, tp),
        P(None, tp),
        P(None, tp),
        P(tp, None),
        P(),
    )
    out_specs = (P(ctx, tp), P(ctx, tp), P(ctx, tp))
    return jax.shard_map(
        local, mesh=split, in_specs=in_specs, out_specs=out_specs, check_vma=False
    )
```
